32 devices in a mesh: groups: 2 (over y), state: 4 (over z), type: 4 (over x, core).
Axes of the slice: x: 2, y: 2, z: 4, core: 2. Of those that a mesh axis runs over, the one named last changes fastest.
Arguments:
- value_in: bfloat16 [16384, 2048], P(('groups', 'state'), 'type'), parts along dimension 0, may hold values from -7.5 to 7.5
- cotangent: bfloat16 [16384, 2048], P(('groups', 'state'), 'type'), parts along dimension 0, may hold values from -100 to 100
- state_util: float32 [2, 16384], P(None, ('groups', 'state')), parts along dimension 1, may hold values from -300 to 300
- taste: float32 [2, 4096], P(None, ('groups', 'type')), parts along dimension 1, may hold values from -6 to 6
- tiles: bfloat16 [128, 2, 6, 128, 128], P(('groups', 'state')), parts along dimension 0, may hold values from 0 to 0.0051879883
- dest_block: int32 [128, 2, 6], P(('groups', 'state')), parts along dimension 0, may hold values from 0 to 63, as said below
- counts: int32 [128, 2], P(('groups', 'state')), parts along dimension 0, may hold values from 1 to 6
Outputs:
- value_out: float32 [16384, 2048], P(('groups', 'state'), 'type'), parts along dimension 0
- adjoint: float32 [16384, 2048], P(('groups', 'state'), 'type'), parts along dimension 0
- grad_util: float32 [2, 16384], P(None, ('groups', 'state')), parts along dimension 1
- grad_taste: float32 [2, 4096], P(None, ('groups', 'type')), parts along dimension 1
The draws below stay inside these ranges and needn't reach their ends.
There are 2 independent parts, one for each index of `groups`. The reference program is written for one: setup_inputs(seed, part) draws one part's arguments, and reference() takes and returns one part's arrays. A program takes and returns all parts, laid end to end along the dimension named above; each array names one. Nothing has to cross between parts.
Inputs may be any that keep to these rules, and one draw needn't show every extreme that they name: `dest_block`: entries at or beyond a list's count name blocks of the list's own run of 16 blocks. In each run of 16 blocks exactly 16 used entries name blocks outside the run, at most 6 of them in any one other run, and exactly 6 in some other run.
All inputs are finite; a program needn't handle non-finite values.
Results may differ from the reference program's by a relative error of at most 0.0012.
Values may be sent and summed in bfloat16 or wider, within the bound.
No kernel may reach another device: no remote copies, remote signals or barrier semaphores. Data moves between devices by JAX's collectives and lax.ppermute only.
A program may use at most 192 MiB of HBM per device.

```python
import math
import jax
import jax.numpy as jnp
from jax import lax

B_DEV = 16
M = 6
TILE = 128
K = 2048
NB = 64
S = 8192
REMOTE = 16
CAP = 6


def integer_lists(key):
    device_count = NB // B_DEV
    entry_total = B_DEV * 2 * M
    list_total = B_DEV * 2
    count_draw = jax.random.randint(jax.random.fold_in(key, 11), (device_count * list_total,), 1, M + 1)
    high_spot = jax.random.randint(jax.random.fold_in(key, 12), (), 0, NB * 2)
    low_spot = (high_spot + 1 + jax.random.randint(jax.random.fold_in(key, 13), (), 0, NB * 2 - 1)) % (NB * 2)
    count_draw = count_draw.at[high_spot].set(M).at[low_spot].set(1)
    count_grid = count_draw.reshape(device_count, list_total)
    entry_pos = jnp.arange(entry_total, dtype=jnp.int32) % M
    list_pos = jnp.arange(entry_total, dtype=jnp.int32) // M
    used = entry_pos[None, :] < count_grid[:, list_pos]
    keys_one = jax.random.split(jax.random.fold_in(key, 14), device_count)
    ranks = jax.vmap(lambda subkey: jax.random.permutation(subkey, entry_total))(keys_one)
    score = ranks + entry_total * (1 - used.astype(jnp.int32))
    chosen = jnp.argsort(score, axis=1, stable=True)[:, :REMOTE]
    pair_total = (device_count - 1) * CAP
    hot_offset = jax.random.randint(jax.random.fold_in(key, 15), (device_count, 1), 1, device_count)
    keys_two = jax.random.split(jax.random.fold_in(key, 16), device_count)
    pair_rank = jax.vmap(lambda subkey: jax.random.permutation(subkey, pair_total))(keys_two)
    offset_of = 1 + jnp.arange(pair_total, dtype=jnp.int32) // CAP
    priority = pair_rank + pair_total * (offset_of[None, :] != hot_offset).astype(jnp.int32)
    pair_pick = jnp.argsort(priority, axis=1, stable=True)[:, :REMOTE]
    device_ids = jnp.arange(device_count, dtype=jnp.int32)[:, None]
    far_owner = (device_ids + 1 + pair_pick // CAP) % device_count
    owners = jnp.broadcast_to(device_ids, (device_count, entry_total))
    rows = jnp.broadcast_to(device_ids, (device_count, REMOTE))
    owners = owners.at[rows, chosen].set(far_owner)
    inner = jax.random.randint(jax.random.fold_in(key, 17), (device_count, entry_total), 0, B_DEV)
    dest = (owners * B_DEV + inner).reshape(NB, 2, M)
    return (dest.astype(jnp.int32), count_grid.reshape(NB, 2).astype(jnp.int32))


def draw_dest_block(key, part):
    return integer_lists(key)[0]


def draw_counts(key, part):
    return integer_lists(key)[1]


def draw_value_in(key, part):
    noise = jnp.clip(jax.random.normal(jax.random.fold_in(key, 1), (S, K), jnp.float32), -6.0, 6.0)
    offset = jax.random.uniform(jax.random.fold_in(key, 2), (NB, 1, 1), jnp.float32, -1.5, 1.5)
    value = (noise.reshape(NB, TILE, K) + offset).reshape(S, K)
    return value.astype(jnp.bfloat16)


def draw_cotangent(key, part):
    offset = jax.random.uniform(jax.random.fold_in(key, 2), (NB, 1, 1), jnp.float32, -1.5, 1.5)
    noise = jnp.clip(jax.random.normal(jax.random.fold_in(key, 1), (S, K), jnp.float32), -6.0, 6.0)
    base = (noise.reshape(NB, TILE, K) + offset).reshape(S, K)
    row_scale = jnp.exp(jax.random.uniform(jax.random.fold_in(key, 4), (S, 1), jnp.float32, 0.0, math.log(10.0)))
    col_scale = jnp.exp(jax.random.uniform(jax.random.fold_in(key, 5), (1, K), jnp.float32, 0.0, math.log(10.0)))
    return (0.1 * base * row_scale * col_scale).astype(jnp.bfloat16)


def draw_state_util(key, part):
    return jnp.clip(jax.random.normal(jax.random.fold_in(key, 1), (2, S), jnp.float32), -6.0, 6.0)


def shard_levels(stream_key, extent, pieces, low, high):
    factor_of = 1.0
    for position, parts in pieces:
        steps = jax.random.uniform(jax.random.fold_in(jax.random.fold_in(stream_key, 6), position), (parts,), jnp.float32, low / len(pieces), high / len(pieces))
        factor_of = factor_of * jnp.repeat(jnp.exp(steps), extent[position] // parts).reshape((-1,) + (1,) * (len(extent) - 1 - position))
    return factor_of


def bell_draw(rng, shape, width, reach, cuts=(), kind=jnp.bfloat16):
    array = jax.random.normal(rng, shape, jnp.float32) * width
    if len(cuts) > 0:
        array = shard_levels(rng, shape, cuts, -0.22, 0.18) * array
    return jnp.clip(array, min=-reach, max=reach).astype(kind)


def setup_inputs(seed: int = 0, part: int = 0) -> dict:
    arg_keys = jax.random.split(jax.random.key(seed), 8)
    part_splits = jax.random.split(jax.random.fold_in(arg_keys[7], part), 8)
    return {
        "value_in": draw_value_in(jax.random.fold_in(jax.random.fold_in(arg_keys[7], part), 71), part),
        "cotangent": draw_cotangent(jax.random.fold_in(jax.random.fold_in(arg_keys[7], part), 71), part),
        "state_util": draw_state_util(jax.random.fold_in(jax.random.fold_in(arg_keys[7], part), 71), part),
        "taste": bell_draw(part_splits[3], (2, K), 1.0, 6.0, ((1, 4),), jnp.float32),
        "tiles": jnp.clip(0.0051879883 * jax.random.uniform(part_splits[4], (NB, 2, M, TILE, TILE), jnp.float32) ** shard_levels(part_splits[4], (NB, 2, M, TILE, TILE), ((0, 4),), -0.2, 0.2), 0.0, 0.0051879883).astype(jnp.bfloat16),
        "dest_block": draw_dest_block(jax.random.fold_in(jax.random.fold_in(arg_keys[7], part), 71), part),
        "counts": draw_counts(jax.random.fold_in(jax.random.fold_in(arg_keys[7], part), 71), part),
    }


def reference(value_in, cotangent, state_util, taste, tiles, dest_block, counts):
    block_count = tiles.shape[0]
    entry_count = tiles.shape[2]
    tile_rows = tiles.shape[3]
    type_width = value_in.shape[1]
    state_count = value_in.shape[0]
    value_blocks = value_in.reshape(block_count, tile_rows, type_width)
    cot_blocks = cotangent.reshape(block_count, tile_rows, type_width)
    util_blocks = state_util.reshape(2, block_count, tile_rows)

    def sweep(carry, block):
        adjoint, taste_total = carry
        tile_here = tiles[block].astype(jnp.float32)
        dest_here = dest_block[block]
        used = jnp.arange(entry_count, dtype=jnp.int32)[None, :] < counts[block][:, None]
        picked = value_blocks[dest_here].astype(jnp.float32) * used[:, :, None, None].astype(jnp.float32)
        cont = jnp.einsum("amij,amjk->aik", tile_here, picked)
        util_here = lax.dynamic_index_in_dim(util_blocks, block, 1, keepdims=False)
        scores = util_here[:, :, None] + taste[:, None, :] + 0.95 * cont
        largest = jnp.max(scores, axis=0)
        value = largest + jnp.log(jnp.sum(jnp.exp(scores - largest[None]), axis=0))
        prob = jnp.exp(scores - value[None])
        grad_q = cot_blocks[block].astype(jnp.float32)[None] * prob
        grad_u = jnp.sum(grad_q, axis=2) / type_width
        scaled = lax.optimization_barrier((0.95 * grad_q).astype(jnp.bfloat16)).astype(jnp.float32)
        contrib = jnp.einsum("amij,aik->amjk", tile_here, scaled)
        contrib = contrib * used[:, :, None, None].astype(jnp.float32)
        remote = (dest_here // B_DEV) != (block // B_DEV)
        rounded = lax.optimization_barrier(contrib.astype(jnp.bfloat16)).astype(jnp.float32)
        contrib = jnp.where(remote[:, :, None, None], rounded, contrib)
        adjoint = adjoint.at[dest_here.reshape(-1)].add(contrib.reshape(-1, tile_rows, type_width))
        taste_total = taste_total + jnp.sum(grad_q, axis=1)
        return (adjoint, taste_total), (value, grad_u)

    start = (jnp.zeros((block_count, tile_rows, type_width), jnp.float32), jnp.zeros((2, type_width), jnp.float32))
    (adjoint, taste_total), (values, grad_units) = lax.scan(sweep, start, jnp.arange(block_count, dtype=jnp.int32))
    value_out = values.reshape(state_count, type_width)
    grad_util = grad_units.transpose(1, 0, 2).reshape(2, state_count)
    grad_taste = taste_total / state_count
    return value_out, adjoint.reshape(state_count, type_width), grad_util, grad_taste
```

```python
import functools

import jax
import jax.numpy as jnp
from jax import lax
from jax.experimental import pallas as pl
from jax.experimental.pallas import tpu as pltpu
from jax.sharding import PartitionSpec as P

DISCOUNT = 0.95
VMEM_LIMIT = 40 * 1024 * 1024

SMEM_SPEC = pl.BlockSpec(memory_space=pltpu.SMEM)
ANY_SPEC = pl.BlockSpec(memory_space=pl.ANY)


def plan_kernel(device_count, capacity, me_ref, dest_ref, counts_ref, req_ref, src_ref, loc_ref, fill_ref):
    block_count, action_count, entry_count = dest_ref.shape
    me = me_ref[0]
    base = me * block_count
    for k in range((device_count - 1) * capacity):
        req_ref[k] = -1
        src_ref[k] = 0
    for k in range(device_count):
        fill_ref[k] = 0

    def one_list(block, action):
        def one_entry(n, carry):
            dest = dest_ref[block, action, n]
            rel = dest - base
            entry = (block * action_count + action) * entry_count + n
            loc_ref[entry] = -1

            @pl.when((rel < 0) | (rel >= block_count))
            def _():
                owner = dest // block_count
                offset = lax.rem(owner - me + device_count, device_count)
                place = fill_ref[offset]
                fill_ref[offset] = place + 1
                slot = (offset - 1) * capacity + place
                req_ref[slot] = dest - owner * block_count
                src_ref[slot] = entry
                loc_ref[entry] = slot

            return carry

        lax.fori_loop(0, counts_ref[block, action], one_entry, 0)

    def one_block(block, carry):
        for action in range(action_count):
            one_list(block, action)
        return carry

    lax.fori_loop(0, block_count, one_block, 0)


def make_plan(me, dest_block, counts, device_count, capacity):
    slots = (device_count - 1) * capacity
    return pl.pallas_call(
        functools.partial(plan_kernel, device_count, capacity),
        out_shape=(
            jax.ShapeDtypeStruct((slots,), jnp.int32),
            jax.ShapeDtypeStruct((slots,), jnp.int32),
            jax.ShapeDtypeStruct((dest_block.size,), jnp.int32),
        ),
        in_specs=[SMEM_SPEC] * 3,
        out_specs=(SMEM_SPEC,) * 3,
        scratch_shapes=[pltpu.SMEM((device_count,), jnp.int32)],
        name="plan",
    )(me, dest_block, counts)


def gather_kernel(wanted_ref, value_ref, out_ref, sems):
    slots = out_ref.shape[0]
    copies = [
        pltpu.make_async_copy(value_ref.at[jnp.maximum(wanted_ref[k], 0)], out_ref.at[k], sems.at[k])
        for k in range(slots)
    ]
    for copy in copies:
        copy.start()
    for copy in copies:
        copy.wait()


def gather_blocks(wanted, value_blocks):
    slots = wanted.shape[0]
    return pl.pallas_call(
        gather_kernel,
        out_shape=jax.ShapeDtypeStruct((slots,) + value_blocks.shape[1:], value_blocks.dtype),
        in_specs=[SMEM_SPEC, ANY_SPEC],
        out_specs=ANY_SPEC,
        scratch_shapes=[pltpu.SemaphoreType.DMA((slots,))],
        cost_estimate=pl.CostEstimate(flops=0, bytes_accessed=1 << 20, transcendentals=0),
        name="gather",
    )(wanted, value_blocks)


def local_forward_kernel(me_ref, dest_ref, counts_ref, value_ref, tiles_ref, util_ref, taste_ref, sent_ref, out_ref, acc_ref):
    del sent_ref
    block = pl.program_id(0)
    _, action_count, entry_count, tile_rows, _ = tiles_ref.shape
    block_count, _, width = value_ref.shape
    base = me_ref[0] * block_count
    for action in range(action_count):
        acc_ref[...] = jnp.zeros_like(acc_ref)
        for n in range(entry_count):
            rel = dest_ref[block, action, n] - base

            @pl.when((n < counts_ref[block, action]) & (rel >= 0) & (rel < block_count))
            def _():
                acc_ref[...] += jnp.dot(
                    tiles_ref[0, action, n], value_ref[rel], preferred_element_type=jnp.float32
                )

        util = jnp.broadcast_to(util_ref[action : action + 1, :], (tile_rows, tile_rows)).T
        taste = taste_ref[action : action + 1, :]
        for c in range(0, width, tile_rows):
            cols = slice(c, c + tile_rows)
            out_ref[0, action, :, cols] = (util + taste[:, cols]) + DISCOUNT * acc_ref[:, cols]


def local_forward(me, dest_block, counts, value_blocks, tiles, state_util, taste, sent):
    block_count, action_count, entry_count, tile_rows, _ = tiles.shape
    width = value_blocks.shape[2]
    return pl.pallas_call(
        local_forward_kernel,
        out_shape=jax.ShapeDtypeStruct((block_count, action_count, tile_rows, width), jnp.float32),
        grid_spec=pltpu.PrefetchScalarGridSpec(
            num_scalar_prefetch=3,
            grid=(block_count,),
            in_specs=[
                pl.BlockSpec(value_blocks.shape, lambda i, *_: (0, 0, 0)),
                pl.BlockSpec((1,) + tiles.shape[1:], lambda i, *_: (i, 0, 0, 0, 0)),
                pl.BlockSpec((action_count, tile_rows), lambda i, *_: (0, i)),
                pl.BlockSpec(taste.shape, lambda i, *_: (0, 0)),
                ANY_SPEC,
            ],
            out_specs=pl.BlockSpec((1, action_count, tile_rows, width), lambda i, *_: (i, 0, 0, 0)),
            scratch_shapes=[pltpu.VMEM((tile_rows, width), jnp.float32)],
        ),
        compiler_params=pltpu.CompilerParams(vmem_limit_bytes=VMEM_LIMIT),
        cost_estimate=pl.CostEstimate(flops=4 * 10**9, bytes_accessed=16 << 20, transcendentals=0),
        name="local_forward",
    )(me, dest_block, counts, value_blocks, tiles, state_util, taste, sent)


def add_remote(block, loc_ref, counts_ref, tiles_ref, incoming_refs, part_ref, scores_ref):
    _, action_count, entry_count, _, _ = tiles_ref.shape
    capacity = incoming_refs[0].shape[0]
    for action in range(action_count):
        scores_ref[action] = part_ref[0, action]
    for action in range(action_count):
        for n in range(entry_count):
            slot = loc_ref[(block * action_count + action) * entry_count + n]
            used = n < counts_ref[block, action]
            for row, incoming_ref in enumerate(incoming_refs):
                place = slot - row * capacity

                @pl.when(used & (place >= 0) & (place < capacity))
                def _():
                    scores_ref[action] += DISCOUNT * jnp.dot(
                        tiles_ref[0, action, n], incoming_ref[place], preferred_element_type=jnp.float32
                    )


def transposed_dot(tile, rows):
    return lax.dot_general(tile, rows, (((0,), (0,)), ((), ())), preferred_element_type=jnp.float32)


def remote_terms_kernel(row_count, src_ref, loc_ref, counts_ref, *refs):
    incoming_refs = refs[:row_count]
    part_ref, tiles_ref, cot_ref, out_ref, scores_ref = refs[row_count:]
    _, action_count, entry_count, _, _ = tiles_ref.shape
    entry = src_ref[pl.program_id(0)]
    one_list = entry // entry_count
    block = one_list // action_count
    action = one_list - block * action_count
    n = entry - one_list * entry_count
    add_remote(block, loc_ref, counts_ref, tiles_ref, incoming_refs, part_ref, scores_ref)
    largest = scores_ref[0]
    for other in range(1, action_count):
        largest = jnp.maximum(largest, scores_ref[other])
    total = jnp.exp(scores_ref[0] - largest)
    for other in range(1, action_count):
        total = total + jnp.exp(scores_ref[other] - largest)
    prob = jnp.exp(scores_ref[action] - largest) / total
    scaled = (DISCOUNT * (cot_ref[0].astype(jnp.float32) * prob)).astype(jnp.bfloat16)
    out_ref[0] = transposed_dot(tiles_ref[0, action, n], scaled).astype(jnp.bfloat16)


def remote_terms(src, loc, counts, incoming, part, tiles, cot_blocks):
    block_count, action_count, entry_count, tile_rows, _ = tiles.shape
    width = cot_blocks.shape[2]
    per_block = action_count * entry_count
    return pl.pallas_call(
        functools.partial(remote_terms_kernel, len(incoming)),
        out_shape=jax.ShapeDtypeStruct((src.shape[0], tile_rows, width), jnp.bfloat16),
        grid_spec=pltpu.PrefetchScalarGridSpec(
            num_scalar_prefetch=3,
            grid=(src.shape[0],),
            in_specs=[pl.BlockSpec(x.shape, lambda r, *_: (0, 0, 0)) for x in incoming]
            + [
                pl.BlockSpec((1,) + part.shape[1:], lambda r, src, *_: (src[r] // per_block, 0, 0, 0)),
                pl.BlockSpec((1,) + tiles.shape[1:], lambda r, src, *_: (src[r] // per_block, 0, 0, 0, 0)),
                pl.BlockSpec((1, tile_rows, width), lambda r, src, *_: (src[r] // per_block, 0, 0)),
            ],
            out_specs=pl.BlockSpec((1, tile_rows, width), lambda r, *_: (r, 0, 0)),
            scratch_shapes=[pltpu.VMEM((action_count, tile_rows, width), jnp.float32)],
        ),
        compiler_params=pltpu.CompilerParams(vmem_limit_bytes=VMEM_LIMIT),
        cost_estimate=pl.CostEstimate(flops=10**8, bytes_accessed=4 << 20, transcendentals=10**5),
        name="remote_terms",
    )(src, loc, counts, *incoming, part, tiles, cot_blocks)


def finish_kernel(row_count, sent_count, util_scale, taste_scale, me_ref, dest_ref, loc_ref, counts_ref, *refs):
    incoming_refs = refs[:row_count]
    part_ref, tiles_ref, cot_ref = refs[row_count : row_count + 3]
    value_ref, adjoint_ref, util_ref, taste_ref, scores_ref, scaled_ref = refs[row_count + 3 + sent_count :]
    block = pl.program_id(0)
    _, action_count, entry_count, tile_rows, _ = tiles_ref.shape
    block_count = adjoint_ref.shape[0]
    width = value_ref.shape[1]
    base = me_ref[0] * block_count

    @pl.when(block == 0)
    def _():
        adjoint_ref[...] = jnp.zeros_like(adjoint_ref)
        taste_ref[...] = jnp.zeros_like(taste_ref)

    add_remote(block, loc_ref, counts_ref, tiles_ref, incoming_refs, part_ref, scores_ref)
    sums = [jnp.zeros((tile_rows, tile_rows), jnp.float32) for _ in range(action_count)]
    for c in range(0, width, tile_rows):
        cols = slice(c, c + tile_rows)
        scores = [scores_ref[action, :, cols] for action in range(action_count)]
        largest = functools.reduce(jnp.maximum, scores)
        powers = [jnp.exp(x - largest) for x in scores]
        total = functools.reduce(jnp.add, powers)
        value_ref[:, cols] = largest + jnp.log(total)
        ratio = cot_ref[0, :, cols].astype(jnp.float32) / total
        for action in range(action_count):
            grad = ratio * powers[action]
            scaled_ref[action, :, cols] = (DISCOUNT * grad).astype(jnp.bfloat16)
            sums[action] = sums[action] + grad
            taste_ref[action : action + 1, cols] += taste_scale * jnp.sum(grad, axis=0, keepdims=True)
    for action in range(action_count):
        util_ref[action : action + 1, :] = util_scale * jnp.sum(sums[action].T, axis=0, keepdims=True)
    for action in range(action_count):
        for n in range(entry_count):
            rel = dest_ref[block, action, n] - base

            @pl.when((n < counts_ref[block, action]) & (rel >= 0) & (rel < block_count))
            def _():
                adjoint_ref[rel] += transposed_dot(tiles_ref[0, action, n], scaled_ref[action])


def finish(me, dest_block, loc, counts, incoming, part, tiles, cot_blocks, sent, util_scale, taste_scale):
    block_count, action_count, entry_count, tile_rows, _ = tiles.shape
    width = cot_blocks.shape[2]
    states = block_count * tile_rows
    return pl.pallas_call(
        functools.partial(finish_kernel, len(incoming), len(sent), util_scale, taste_scale),
        out_shape=(
            jax.ShapeDtypeStruct((states, width), jnp.float32),
            jax.ShapeDtypeStruct((block_count, tile_rows, width), jnp.float32),
            jax.ShapeDtypeStruct((action_count, states), jnp.float32),
            jax.ShapeDtypeStruct((action_count, width), jnp.float32),
        ),
        grid_spec=pltpu.PrefetchScalarGridSpec(
            num_scalar_prefetch=4,
            grid=(block_count,),
            in_specs=[pl.BlockSpec(x.shape, lambda i, *_: (0, 0, 0)) for x in incoming]
            + [
                pl.BlockSpec((1,) + part.shape[1:], lambda i, *_: (i, 0, 0, 0)),
                pl.BlockSpec((1,) + tiles.shape[1:], lambda i, *_: (i, 0, 0, 0, 0)),
                pl.BlockSpec((1, tile_rows, width), lambda i, *_: (i, 0, 0)),
            ]
            + [ANY_SPEC] * len(sent),
            out_specs=(
                pl.BlockSpec((tile_rows, width), lambda i, *_: (i, 0)),
                pl.BlockSpec((block_count, tile_rows, width), lambda i, *_: (0, 0, 0)),
                pl.BlockSpec((action_count, tile_rows), lambda i, *_: (0, i)),
                pl.BlockSpec((action_count, width), lambda i, *_: (0, 0)),
            ),
            scratch_shapes=[
                pltpu.VMEM((action_count, tile_rows, width), jnp.float32),
                pltpu.VMEM((action_count, tile_rows, width), jnp.bfloat16),
            ],
        ),
        compiler_params=pltpu.CompilerParams(vmem_limit_bytes=VMEM_LIMIT),
        cost_estimate=pl.CostEstimate(flops=4 * 10**9, bytes_accessed=24 << 20, transcendentals=4 * 10**6),
        name="finish",
    )(me, dest_block, loc, counts, *incoming, part, tiles, cot_blocks, *sent)


def add_arrivals_kernel(wanted_ref, arrived_ref, base_ref, out_ref, held_ref, in_sems, out_sems):
    slots = arrived_ref.shape[0]
    target = [wanted_ref[k] for k in range(slots)]
    lead = []
    for k in range(slots):
        first = target[k] >= 0
        for other in range(k):
            first = first & (target[other] != target[k])
        lead.append(first)
    place = [jnp.maximum(t, 0) for t in target]
    fetch = [pltpu.make_async_copy(out_ref.at[place[k]], held_ref.at[k], in_sems.at[k]) for k in range(slots)]
    store = [pltpu.make_async_copy(held_ref.at[k], out_ref.at[place[k]], out_sems.at[k]) for k in range(slots)]
    for k in range(slots):

        @pl.when(lead[k])
        def _():
            fetch[k].start()

    for k in range(slots):

        @pl.when(lead[k])
        def _():
            fetch[k].wait()
            held_ref[k] += arrived_ref[k].astype(jnp.float32)
            for other in range(k + 1, slots):

                @pl.when(target[other] == target[k])
                def _():
                    held_ref[k] += arrived_ref[other].astype(jnp.float32)

            store[k].start()

    for k in range(slots):

        @pl.when(lead[k])
        def _():
            store[k].wait()


def add_arrivals(wanted, arrived, adjoint):
    slots = arrived.shape[0]
    return pl.pallas_call(
        add_arrivals_kernel,
        out_shape=jax.ShapeDtypeStruct(adjoint.shape, adjoint.dtype),
        in_specs=[SMEM_SPEC, pl.BlockSpec(memory_space=pltpu.VMEM), ANY_SPEC],
        out_specs=ANY_SPEC,
        scratch_shapes=[
            pltpu.VMEM(arrived.shape, jnp.float32),
            pltpu.SemaphoreType.DMA((slots,)),
            pltpu.SemaphoreType.DMA((slots,)),
        ],
        input_output_aliases={2: 0},
        compiler_params=pltpu.CompilerParams(vmem_limit_bytes=VMEM_LIMIT),
        cost_estimate=pl.CostEstimate(flops=10**6, bytes_accessed=4 << 20, transcendentals=0),
        name="add_arrivals",
    )(wanted, arrived, adjoint)


def local(value_in, cotangent, state_util, taste, tiles, dest_block, counts):
    block_count, action_count, entry_count, tile_rows, _ = tiles.shape
    width = value_in.shape[1]
    device_count = lax.axis_size("state")
    me = lax.axis_index("state").astype(jnp.int32).reshape(1)
    capacity = max(2, (block_count + device_count - 2) // (device_count - 1))
    value_blocks = value_in.reshape(block_count, tile_rows, width)
    cot_blocks = cotangent.reshape(block_count, tile_rows, width)
    offsets = range(1, device_count)
    order = sorted(offsets, key=lambda d: -min(d, device_count - d))

    def shift(x, offset):
        return lax.ppermute(x, "state", [(s, (s + offset) % device_count) for s in range(device_count)])

    def row(x, offset):
        return lax.slice(x, ((offset - 1) * capacity,), (offset * capacity,))

    request, source, loc = make_plan(me, dest_block, counts, device_count, capacity)
    wanted = {d: shift(row(request, d), d) for d in order}
    outgoing = {d: gather_blocks(wanted[d], value_blocks) for d in order}
    incoming = {d: shift(outgoing[d], -d) for d in order}
    part = local_forward(me, dest_block, counts, value_blocks, tiles, state_util, taste, outgoing[order[-1]])
    held = [incoming[d] for d in offsets]

    returned = []
    sent = []
    for index, d in enumerate(order):
        cuts = [0, min(2, capacity), capacity] if index == 0 else [0, capacity]
        for lo, hi in zip(cuts[:-1], cuts[1:]):
            if lo < hi:
                src = row(source, d)[lo:hi]
                terms = remote_terms(src, loc, counts, held, part, tiles, cot_blocks)
                sent.append(terms)
                returned.append((wanted[d][lo:hi], shift(terms, d)))
    value_out, adjoint, util_part, taste_part = finish(
        me, dest_block, loc, counts, held, part, tiles, cot_blocks, sent,
        1.0 / (width * lax.axis_size("type")), 1.0 / (block_count * tile_rows * device_count),
    )
    util_total = lax.psum(util_part, "type")
    taste_total = lax.psum(taste_part, "state")
    for places, terms in returned:
        adjoint = add_arrivals(places, terms, adjoint)
    return value_out, adjoint.reshape(block_count * tile_rows, width), util_total, taste_total


def solution(mesh):
    return jax.shard_map(
        local,
        mesh=mesh,
        in_specs=(
            P(("groups", "state"), "type"),
            P(("groups", "state"), "type"),
            P(None, ("groups", "state")),
            P(None, ("groups", "type")),
            P(("groups", "state"), None, None, None, None),
            P(("groups", "state"), None, None),
            P(("groups", "state"), None),
        ),
        out_specs=(
            P(("groups", "state"), "type"),
            P(("groups", "state"), "type"),
            P(None, ("groups", "state")),
            P(None, ("groups", "type")),
        ),
        check_vma=False,
    )
```

```python
import functools

import jax
import jax.numpy as jnp
from jax import lax
from jax.experimental import pallas as pl
from jax.experimental.pallas import tpu as pltpu
from jax.sharding import PartitionSpec as P

DISCOUNT = 0.95
VMEM_LIMIT = 40 * 1024 * 1024

SMEM_SPEC = pl.BlockSpec(memory_space=pltpu.SMEM)
ANY_SPEC = pl.BlockSpec(memory_space=pl.ANY)


def dot_f32(x, y, contract=(1, 0)):
    return lax.dot_general(
        x, y, (((contract[0],), (contract[1],)), ((), ())),
        precision=lax.Precision.HIGHEST, preferred_element_type=jnp.float32,
    )


def iota(shape, dim):
    return lax.broadcasted_iota(jnp.int32, shape, dim)


def plan_kernel(device_count, me_ref, dest_ref, counts_ref, *refs):
    request_refs = refs[: device_count - 1]
    source_refs = refs[device_count - 1 : 2 * (device_count - 1)]
    slot_ref, local_ref, mark_ref = refs[2 * (device_count - 1) :]
    entry_count, action_count, block_count = dest_ref.shape
    capacity = request_refs[0].shape[1]
    rows, places = slot_ref.shape[0], 8 * pl.cdiv(capacity, 8)
    me = me_ref[0]
    mark_ref[...] = jnp.zeros_like(mark_ref)
    local_ref[...] = jnp.zeros_like(local_ref)
    for n in range(entry_count):
        dest = dest_ref[n]
        owner = jnp.zeros_like(dest)
        for other in range(1, device_count):
            owner += (dest >= other * block_count).astype(jnp.int32)
        offset = owner - me
        offset = jnp.where(offset < 0, offset + device_count, offset)
        mark = jnp.where(n < counts_ref[...], offset, 0)
        mark_ref[n * action_count : (n + 1) * action_count, :] = mark
        local_ref[n * action_count : (n + 1) * action_count, :] = dest - owner * block_count
    mark, local = mark_ref[...], local_ref[...]
    row, lane = iota(mark.shape, 0), iota(mark.shape, 1)
    entry = row // action_count
    code = lane * 256 + (row - entry * action_count) * 16 + entry
    square = (block_count, block_count)
    before = (iota(square, 0) < iota(square, 1)).astype(jnp.float32)
    whole = jnp.ones(square, jnp.float32)
    tall = (mark.shape[0],) * 2
    above = (iota(tall, 1) < iota(tall, 0)).astype(jnp.float32)
    ones = jnp.ones((8, block_count), jnp.float32)
    slot = jnp.full(mark.shape, -1, jnp.int32)
    place_iota = iota((places, block_count), 0)
    for offset in range(1, device_count):
        hit = mark == offset
        hits = hit.astype(jnp.float32)
        place = (dot_f32(hits, before) + dot_f32(above, dot_f32(hits, whole))).astype(jnp.int32)
        slot = jnp.where(hit, (offset - 1) * capacity + place, slot)
        place = jnp.where(hit, place, -1)
        wants = jnp.zeros((places, block_count), jnp.int32)
        codes = jnp.zeros((places, block_count), jnp.int32)
        for r in range(entry_count * action_count):
            here = place[r : r + 1, :] == place_iota
            wants = jnp.where(here, local[r : r + 1, :] + 1, wants)
            codes = jnp.where(here, code[r : r + 1, :], codes)
        wants = dot_f32(ones, wants.astype(jnp.float32), (1, 1)).astype(jnp.int32) - 1
        codes = dot_f32(ones, codes.astype(jnp.float32), (1, 1)).astype(jnp.int32)
        request_refs[offset - 1][...] = wants[:1, :capacity]
        source_refs[offset - 1][...] = codes[:1, :capacity]
    slot_ref[...] = slot[:rows]


def make_plan(me, dest, counts, device_count, capacity):
    entry_count, action_count, block_count = dest.shape
    rows = entry_count * action_count
    padded = 8 * pl.cdiv(rows, 8)
    vmem = pl.BlockSpec(memory_space=pltpu.VMEM)
    outs = pl.pallas_call(
        functools.partial(plan_kernel, device_count),
        out_shape=[jax.ShapeDtypeStruct((1, capacity), jnp.int32)] * (2 * (device_count - 1))
        + [jax.ShapeDtypeStruct((rows, block_count), jnp.int32)],
        in_specs=[SMEM_SPEC, vmem, vmem],
        out_specs=[vmem] * (2 * device_count - 1),
        scratch_shapes=[pltpu.VMEM((padded, block_count), jnp.int32)] * 2,
        name="plan",
    )(me, dest, counts)
    return outs[: device_count - 1], outs[device_count - 1 : -1], outs[-1]


def gather_kernel(wanted_ref, value_ref, out_ref):
    del wanted_ref
    out_ref[...] = value_ref[...]


def gather_blocks(wanted, value_blocks):
    capacity = wanted.shape[1]
    block = (1,) + value_blocks.shape[1:]
    return pl.pallas_call(
        gather_kernel,
        out_shape=jax.ShapeDtypeStruct((capacity,) + value_blocks.shape[1:], value_blocks.dtype),
        grid_spec=pltpu.PrefetchScalarGridSpec(
            num_scalar_prefetch=1,
            grid=(capacity,),
            in_specs=[pl.BlockSpec(block, lambda k, wanted: (jnp.maximum(wanted[0, k], 0), 0, 0))],
            out_specs=pl.BlockSpec(block, lambda k, wanted: (k, 0, 0)),
        ),
        cost_estimate=pl.CostEstimate(flops=0, bytes_accessed=1 << 20, transcendentals=0),
        name="gather",
    )(wanted, value_blocks)


def local_forward_kernel(me_ref, dest_ref, counts_ref, value_ref, tiles_ref, util_ref, taste_ref, sent_ref, out_ref, acc_ref):
    del sent_ref
    block = pl.program_id(0)
    _, action_count, entry_count, tile_rows, _ = tiles_ref.shape
    block_count, _, width = value_ref.shape
    base = me_ref[0] * block_count
    for action in range(action_count):
        acc_ref[...] = jnp.zeros_like(acc_ref)
        for n in range(entry_count):
            rel = dest_ref[n, action, block] - base

            @pl.when((n < counts_ref[action, block]) & (rel >= 0) & (rel < block_count))
            def _():
                acc_ref[...] += jnp.dot(
                    tiles_ref[0, action, n], value_ref[rel], preferred_element_type=jnp.float32
                )

        util = jnp.broadcast_to(util_ref[action : action + 1, :], (tile_rows, tile_rows)).T
        taste = taste_ref[action : action + 1, :]
        for c in range(0, width, tile_rows):
            cols = slice(c, c + tile_rows)
            out_ref[0, action, :, cols] = (util + taste[:, cols]) + DISCOUNT * acc_ref[:, cols]


def local_forward(me, dest, counts, value_blocks, tiles, state_util, taste, sent):
    block_count, action_count, entry_count, tile_rows, _ = tiles.shape
    width = value_blocks.shape[2]
    return pl.pallas_call(
        local_forward_kernel,
        out_shape=jax.ShapeDtypeStruct((block_count, action_count, tile_rows, width), jnp.float32),
        grid_spec=pltpu.PrefetchScalarGridSpec(
            num_scalar_prefetch=3,
            grid=(block_count,),
            in_specs=[
                pl.BlockSpec(value_blocks.shape, lambda i, *_: (0, 0, 0)),
                pl.BlockSpec((1,) + tiles.shape[1:], lambda i, *_: (i, 0, 0, 0, 0)),
                pl.BlockSpec((action_count, tile_rows), lambda i, *_: (0, i)),
                pl.BlockSpec(taste.shape, lambda i, *_: (0, 0)),
                ANY_SPEC,
            ],
            out_specs=pl.BlockSpec((1, action_count, tile_rows, width), lambda i, *_: (i, 0, 0, 0)),
            scratch_shapes=[pltpu.VMEM((tile_rows, width), jnp.float32)],
        ),
        compiler_params=pltpu.CompilerParams(vmem_limit_bytes=VMEM_LIMIT),
        cost_estimate=pl.CostEstimate(flops=4 * 10**9, bytes_accessed=16 << 20, transcendentals=0),
        name="local_forward",
    )(me, dest, counts, value_blocks, tiles, state_util, taste, sent)


def add_remote(block, slot_ref, tiles_ref, incoming_refs, part_ref, scores_ref):
    _, action_count, entry_count, _, _ = tiles_ref.shape
    capacity = incoming_refs[0].shape[0]
    for action in range(action_count):
        scores_ref[action] = part_ref[0, action]
    for action in range(action_count):
        for n in range(entry_count):
            slot = slot_ref[n * action_count + action, block]

            @pl.when(slot >= 0)
            def _():
                for row, incoming_ref in enumerate(incoming_refs):
                    place = slot - row * capacity

                    @pl.when((place >= 0) & (place < capacity))
                    def _():
                        scores_ref[action] += DISCOUNT * jnp.dot(
                            tiles_ref[0, action, n], incoming_ref[place], preferred_element_type=jnp.float32
                        )


def transposed_dot(tile, rows):
    return lax.dot_general(tile, rows, (((0,), (0,)), ((), ())), preferred_element_type=jnp.float32)


def remote_terms_kernel(row_count, sent_count, src_ref, slot_ref, *refs):
    incoming_refs = refs[:row_count]
    part_ref, tiles_ref, cot_ref = refs[row_count : row_count + 3]
    out_ref, scores_ref, scaled_ref = refs[row_count + 3 + sent_count :]
    _, action_count, _, tile_rows, _ = tiles_ref.shape
    width = cot_ref.shape[2]
    code = src_ref[0, pl.program_id(0)]
    block, action, n = code >> 8, (code >> 4) & 15, code & 15
    add_remote(block, slot_ref, tiles_ref, incoming_refs, part_ref, scores_ref)
    for c in range(0, width, tile_rows):
        cols = slice(c, c + tile_rows)
        scores = [scores_ref[other, :, cols] for other in range(action_count)]
        largest = functools.reduce(jnp.maximum, scores)
        total = functools.reduce(jnp.add, [jnp.exp(x - largest) for x in scores])
        ratio = cot_ref[0, :, cols].astype(jnp.float32) / total
        grad = ratio * jnp.exp(scores_ref[action, :, cols] - largest)
        scaled_ref[:, cols] = (DISCOUNT * grad).astype(jnp.bfloat16)
    out_ref[0] = transposed_dot(tiles_ref[0, action, n], scaled_ref[...]).astype(jnp.bfloat16)


def remote_terms(src, slot, incoming, part, tiles, cot_blocks, sent):
    _, action_count, entry_count, tile_rows, _ = tiles.shape
    width = cot_blocks.shape[2]
    count = src.shape[1]
    return pl.pallas_call(
        functools.partial(remote_terms_kernel, len(incoming), len(sent)),
        out_shape=jax.ShapeDtypeStruct((count, tile_rows, width), jnp.bfloat16),
        grid_spec=pltpu.PrefetchScalarGridSpec(
            num_scalar_prefetch=2,
            grid=(count,),
            in_specs=[pl.BlockSpec(x.shape, lambda r, *_: (0, 0, 0)) for x in incoming]
            + [
                pl.BlockSpec((1,) + part.shape[1:], lambda r, src, *_: (src[0, r] >> 8, 0, 0, 0)),
                pl.BlockSpec((1,) + tiles.shape[1:], lambda r, src, *_: (src[0, r] >> 8, 0, 0, 0, 0)),
                pl.BlockSpec((1, tile_rows, width), lambda r, src, *_: (src[0, r] >> 8, 0, 0)),
            ]
            + [ANY_SPEC] * len(sent),
            out_specs=pl.BlockSpec((1, tile_rows, width), lambda r, *_: (r, 0, 0)),
            scratch_shapes=[
                pltpu.VMEM((action_count, tile_rows, width), jnp.float32),
                pltpu.VMEM((tile_rows, width), jnp.bfloat16),
            ],
        ),
        compiler_params=pltpu.CompilerParams(vmem_limit_bytes=VMEM_LIMIT),
        cost_estimate=pl.CostEstimate(flops=10**8, bytes_accessed=4 << 20, transcendentals=10**5),
        name="remote_terms",
    )(src, slot, *incoming, part, tiles, cot_blocks, *sent)


def finish_kernel(row_count, sent_count, util_scale, taste_scale, me_ref, dest_ref, slot_ref, counts_ref, *refs):
    incoming_refs = refs[:row_count]
    part_ref, tiles_ref, cot_ref = refs[row_count : row_count + 3]
    value_ref, adjoint_ref, util_ref, taste_ref, scores_ref, scaled_ref = refs[row_count + 3 + sent_count :]
    block = pl.program_id(0)
    _, action_count, entry_count, tile_rows, _ = tiles_ref.shape
    block_count = adjoint_ref.shape[0]
    width = value_ref.shape[1]
    base = me_ref[0] * block_count

    @pl.when(block == 0)
    def _():
        adjoint_ref[...] = jnp.zeros_like(adjoint_ref)
        taste_ref[...] = jnp.zeros_like(taste_ref)

    add_remote(block, slot_ref, tiles_ref, incoming_refs, part_ref, scores_ref)
    sums = [jnp.zeros((tile_rows, tile_rows), jnp.float32) for _ in range(action_count)]
    for c in range(0, width, tile_rows):
        cols = slice(c, c + tile_rows)
        scores = [scores_ref[action, :, cols] for action in range(action_count)]
        largest = functools.reduce(jnp.maximum, scores)
        powers = [jnp.exp(x - largest) for x in scores]
        total = functools.reduce(jnp.add, powers)
        value_ref[:, cols] = largest + jnp.log(total)
        ratio = cot_ref[0, :, cols].astype(jnp.float32) / total
        for action in range(action_count):
            grad = ratio * powers[action]
            scaled_ref[action, :, cols] = (DISCOUNT * grad).astype(jnp.bfloat16)
            sums[action] = sums[action] + grad
            taste_ref[action : action + 1, cols] += taste_scale * jnp.sum(grad, axis=0, keepdims=True)
    for action in range(action_count):
        util_ref[action : action + 1, :] = util_scale * jnp.sum(sums[action].T, axis=0, keepdims=True)
    for action in range(action_count):
        for n in range(entry_count):
            rel = dest_ref[n, action, block] - base

            @pl.when((n < counts_ref[action, block]) & (rel >= 0) & (rel < block_count))
            def _():
                adjoint_ref[rel] += transposed_dot(tiles_ref[0, action, n], scaled_ref[action])


def finish(me, dest, slot, counts, incoming, part, tiles, cot_blocks, sent, util_scale, taste_scale):
    block_count, action_count, entry_count, tile_rows, _ = tiles.shape
    width = cot_blocks.shape[2]
    states = block_count * tile_rows
    return pl.pallas_call(
        functools.partial(finish_kernel, len(incoming), len(sent), util_scale, taste_scale),
        out_shape=(
            jax.ShapeDtypeStruct((states, width), jnp.float32),
            jax.ShapeDtypeStruct((block_count, tile_rows, width), jnp.float32),
            jax.ShapeDtypeStruct((action_count, states), jnp.float32),
            jax.ShapeDtypeStruct((action_count, width), jnp.float32),
        ),
        grid_spec=pltpu.PrefetchScalarGridSpec(
            num_scalar_prefetch=4,
            grid=(block_count,),
            in_specs=[pl.BlockSpec(x.shape, lambda i, *_: (0, 0, 0)) for x in incoming]
            + [
                pl.BlockSpec((1,) + part.shape[1:], lambda i, *_: (i, 0, 0, 0)),
                pl.BlockSpec((1,) + tiles.shape[1:], lambda i, *_: (i, 0, 0, 0, 0)),
                pl.BlockSpec((1, tile_rows, width), lambda i, *_: (i, 0, 0)),
            ]
            + [ANY_SPEC] * len(sent),
            out_specs=(
                pl.BlockSpec((tile_rows, width), lambda i, *_: (i, 0)),
                pl.BlockSpec((block_count, tile_rows, width), lambda i, *_: (0, 0, 0)),
                pl.BlockSpec((action_count, tile_rows), lambda i, *_: (0, i)),
                pl.BlockSpec((action_count, width), lambda i, *_: (0, 0)),
            ),
            scratch_shapes=[
                pltpu.VMEM((action_count, tile_rows, width), jnp.float32),
                pltpu.VMEM((action_count, tile_rows, width), jnp.bfloat16),
            ],
        ),
        compiler_params=pltpu.CompilerParams(vmem_limit_bytes=VMEM_LIMIT),
        cost_estimate=pl.CostEstimate(flops=4 * 10**9, bytes_accessed=24 << 20, transcendentals=4 * 10**6),
        name="finish",
    )(me, dest, slot, counts, *incoming, part, tiles, cot_blocks, *sent)


def add_arrivals_kernel(wanted_ref, arrived_ref, base_ref, out_ref, held_ref, in_sems, out_sems):
    slots = arrived_ref.shape[0]
    target = [wanted_ref[0, k] for k in range(slots)]
    lead = []
    for k in range(slots):
        first = target[k] >= 0
        for other in range(k):
            first = first & (target[other] != target[k])
        lead.append(first)
    place = [jnp.maximum(t, 0) for t in target]
    fetch = [pltpu.make_async_copy(out_ref.at[place[k]], held_ref.at[k], in_sems.at[k]) for k in range(slots)]
    store = [pltpu.make_async_copy(held_ref.at[k], out_ref.at[place[k]], out_sems.at[k]) for k in range(slots)]
    for k in range(slots):

        @pl.when(lead[k])
        def _():
            fetch[k].start()

    for k in range(slots):

        @pl.when(lead[k])
        def _():
            fetch[k].wait()
            held_ref[k] += arrived_ref[k].astype(jnp.float32)
            for other in range(k + 1, slots):

                @pl.when(target[other] == target[k])
                def _():
                    held_ref[k] += arrived_ref[other].astype(jnp.float32)

            store[k].start()

    for k in range(slots):

        @pl.when(lead[k])
        def _():
            store[k].wait()


def add_arrivals(wanted, arrived, adjoint):
    slots = arrived.shape[0]
    return pl.pallas_call(
        add_arrivals_kernel,
        out_shape=jax.ShapeDtypeStruct(adjoint.shape, adjoint.dtype),
        in_specs=[SMEM_SPEC, pl.BlockSpec(memory_space=pltpu.VMEM), ANY_SPEC],
        out_specs=ANY_SPEC,
        scratch_shapes=[
            pltpu.VMEM(arrived.shape, jnp.float32),
            pltpu.SemaphoreType.DMA((slots,)),
            pltpu.SemaphoreType.DMA((slots,)),
        ],
        input_output_aliases={2: 0},
        compiler_params=pltpu.CompilerParams(vmem_limit_bytes=VMEM_LIMIT),
        cost_estimate=pl.CostEstimate(flops=10**6, bytes_accessed=4 << 20, transcendentals=0),
        name="add_arrivals",
    )(wanted, arrived, adjoint)


def local(value_in, cotangent, state_util, taste, tiles, dest_block, counts):
    block_count, action_count, entry_count, tile_rows, _ = tiles.shape
    width = value_in.shape[1]
    device_count = lax.axis_size("state")
    me = lax.axis_index("state").astype(jnp.int32).reshape(1)
    capacity = max(2, (block_count + device_count - 2) // (device_count - 1))
    value_blocks = value_in.reshape(block_count, tile_rows, width)
    cot_blocks = cotangent.reshape(block_count, tile_rows, width)
    offsets = range(1, device_count)
    order = sorted(offsets, key=lambda d: -min(d, device_count - d))

    def shift(x, offset):
        return lax.ppermute(x, "state", [(s, (s + offset) % device_count) for s in range(device_count)])

    def add_over(x, axis):
        size = lax.axis_size(axis)
        if size & (size - 1):
            return lax.psum(x, axis)
        step = 1
        while step < size:
            x = x + lax.ppermute(x, axis, [(s, s ^ step) for s in range(size)])
            step *= 2
        return x

    dest, counts = dest_block.transpose(2, 1, 0), counts.T
    request, source, slot = make_plan(me, dest, counts, device_count, capacity)
    wanted = {d: shift(request[d - 1], d) for d in order}
    outgoing = {d: gather_blocks(wanted[d], value_blocks) for d in order}
    incoming = {d: shift(outgoing[d], -d) for d in order}
    part = local_forward(me, dest, counts, value_blocks, tiles, state_util, taste, outgoing[order[-1]])
    held = [incoming[d] for d in offsets]

    returned = []
    sent = []
    for index, d in enumerate(order):
        cuts = [0, min(2, capacity), capacity] if index == 0 else [0, capacity]
        for lo, hi in zip(cuts[:-1], cuts[1:]):
            if lo < hi:
                terms = remote_terms(source[d - 1][:, lo:hi], slot, held, part, tiles, cot_blocks, sent[-1:])
                sent.append(terms)
                returned.append((wanted[d][:, lo:hi], shift(terms, d)))
    value_out, adjoint, util_part, taste_part = finish(
        me, dest, slot, counts, held, part, tiles, cot_blocks, sent,
        1.0 / (width * lax.axis_size("type")), 1.0 / (block_count * tile_rows * device_count),
    )
    util_total = add_over(util_part, "type")
    taste_total = add_over(taste_part, "state")
    for places, terms in returned:
        adjoint = add_arrivals(places, terms, adjoint)
    return value_out, adjoint.reshape(block_count * tile_rows, width), util_total, taste_total


def solution(mesh):
    return jax.shard_map(
        local,
        mesh=mesh,
        in_specs=(
            P(("groups", "state"), "type"),
            P(("groups", "state"), "type"),
            P(None, ("groups", "state")),
            P(None, ("groups", "type")),
            P(("groups", "state"), None, None, None, None),
            P(("groups", "state"), None, None),
            P(("groups", "state"), None),
        ),
        out_specs=(
            P(("groups", "state"), "type"),
            P(("groups", "state"), "type"),
            P(None, ("groups", "state")),
            P(None, ("groups", "type")),
        ),
        check_vma=False,
    )
```

```python
import functools

import jax
import jax.numpy as jnp
from jax import lax
from jax.experimental import pallas as pl
from jax.experimental.pallas import tpu as pltpu
from jax.sharding import PartitionSpec as P

DISCOUNT = 0.95
VMEM_LIMIT = 12 * 1024 * 1024

SMEM_SPEC = pl.BlockSpec(memory_space=pltpu.SMEM)
ANY_SPEC = pl.BlockSpec(memory_space=pl.ANY)
HBM_SPEC = pl.BlockSpec(memory_space=pltpu.HBM)
VMEM_SPEC = pl.BlockSpec(memory_space=pltpu.VMEM)
PARAMS = pltpu.CompilerParams(vmem_limit_bytes=VMEM_LIMIT)
SMALL_COST = pl.CostEstimate(flops=1000, bytes_accessed=1000, transcendentals=0)


def dot_counts(x, y, contract=(1, 0)):
    return lax.dot_general(
        x.astype(jnp.float32).astype(jnp.bfloat16), y.astype(jnp.float32).astype(jnp.bfloat16),
        (((contract[0],), (contract[1],)), ((), ())), preferred_element_type=jnp.float32,
    )


def iota(shape, dim):
    return lax.broadcasted_iota(jnp.int32, shape, dim)


def plan_kernel(device_count, me_ref, dest_hbm_ref, counts_hbm_ref, *refs):
    request_refs = refs[: device_count - 1]
    source_refs = refs[device_count - 1 : 2 * (device_count - 1)]
    dest_ref, counts_ref, mark_ref, local_ref, sems = refs[2 * (device_count - 1) :]
    copies = [
        pltpu.make_async_copy(dest_hbm_ref, dest_ref, sems.at[0]),
        pltpu.make_async_copy(counts_hbm_ref, counts_ref, sems.at[1]),
    ]
    for copy in copies:
        copy.start()
    entry_count, action_count, block_count = dest_ref.shape
    capacity = request_refs[0].shape[1]
    places = 8 * pl.cdiv(capacity, 8)
    me = me_ref[0]
    mark_ref[...] = jnp.zeros_like(mark_ref)
    local_ref[...] = jnp.zeros_like(local_ref)
    for copy in copies:
        copy.wait()
    for n in range(entry_count):
        dest = dest_ref[n]
        owner = jnp.zeros_like(dest)
        for other in range(1, device_count):
            owner += (dest >= other * block_count).astype(jnp.int32)
        offset = owner - me
        offset = jnp.where(offset < 0, offset + device_count, offset)
        mark = jnp.where(n < counts_ref[...], offset, 0)
        mark_ref[n * action_count : (n + 1) * action_count, :] = mark
        local_ref[n * action_count : (n + 1) * action_count, :] = dest - owner * block_count
    mark, local = mark_ref[...], local_ref[...]
    row, lane = iota(mark.shape, 0), iota(mark.shape, 1)
    square = (block_count, block_count)
    before = iota(square, 0) < iota(square, 1)
    whole = jnp.ones(square, jnp.int32)
    tall = (mark.shape[0],) * 2
    above = iota(tall, 1) < iota(tall, 0)
    ones = jnp.ones((8, block_count), jnp.int32)
    place_iota = iota((places, block_count), 0)
    for offset in range(1, device_count):
        hit = mark == offset
        place = (dot_counts(hit, before) + dot_counts(above, dot_counts(hit, whole))).astype(jnp.int32)
        place = jnp.where(hit, place, -1)
        wants = jnp.zeros((places, block_count), jnp.int32)
        blocks = jnp.zeros((places, block_count), jnp.int32)
        lists = jnp.zeros((places, block_count), jnp.int32)
        for r in range(entry_count * action_count):
            here = place[r : r + 1, :] == place_iota
            wants = jnp.where(here, local[r : r + 1, :] + 1, wants)
            blocks = jnp.where(here, lane[r : r + 1, :], blocks)
            lists = jnp.where(here, row[r : r + 1, :], lists)
        wants, blocks, lists = (dot_counts(ones, x, (1, 1)).astype(jnp.int32) for x in (wants, blocks, lists))
        entry = lists // action_count
        codes = jnp.where(wants > 0, blocks * 256 + (lists - entry * action_count) * 16 + entry, -1)
        request_refs[offset - 1][...] = (wants - 1)[:1, :capacity]
        source_refs[offset - 1][...] = codes[:1, :capacity]


def make_plan(me, dest, counts, device_count, capacity):
    entry_count, action_count, block_count = dest.shape
    padded = 8 * pl.cdiv(entry_count * action_count, 8)
    outs = pl.pallas_call(
        functools.partial(plan_kernel, device_count),
        out_shape=[jax.ShapeDtypeStruct((1, capacity), jnp.int32)] * (2 * (device_count - 1)),
        in_specs=[SMEM_SPEC, HBM_SPEC, HBM_SPEC],
        out_specs=[VMEM_SPEC] * (2 * (device_count - 1)),
        scratch_shapes=[pltpu.VMEM(dest.shape, jnp.int32), pltpu.VMEM(counts.shape, jnp.int32)]
        + [pltpu.VMEM((padded, block_count), jnp.int32)] * 2
        + [pltpu.SemaphoreType.DMA((2,))],
        compiler_params=PARAMS,
        cost_estimate=SMALL_COST,
        name="plan",
    )(me, dest, counts)
    return outs[: device_count - 1], outs[device_count - 1 :]


def stage_kernel(value_ref, plan_ref, out_ref):
    del plan_ref
    for block in range(out_ref.shape[0]):
        out_ref[block] = value_ref[block]


def stage(value_blocks, plan):
    return pl.pallas_call(
        stage_kernel,
        out_shape=jax.ShapeDtypeStruct(value_blocks.shape, value_blocks.dtype),
        in_specs=[VMEM_SPEC, ANY_SPEC],
        out_specs=VMEM_SPEC,
        compiler_params=PARAMS,
        cost_estimate=SMALL_COST,
        name="stage",
    )(value_blocks, plan)


def gather_kernel(wanted_ref, value_ref, out_ref):
    for k in range(out_ref.shape[0]):
        out_ref[k] = value_ref[jnp.maximum(wanted_ref[0, k], 0)]


def gather_blocks(wanted, value_blocks):
    return pl.pallas_call(
        gather_kernel,
        out_shape=jax.ShapeDtypeStruct(wanted.shape[1:] + value_blocks.shape[1:], value_blocks.dtype),
        in_specs=[SMEM_SPEC, VMEM_SPEC],
        out_specs=VMEM_SPEC,
        compiler_params=PARAMS,
        cost_estimate=SMALL_COST,
        name="gather",
    )(wanted, value_blocks)


def local_forward_kernel(me_ref, dest_ref, counts_ref, value_ref, tiles_ref, util_ref, taste_ref, sent_ref, out_ref):
    del sent_ref
    block_count, action_count, entry_count, tile_rows, _ = tiles_ref.shape
    width = value_ref.shape[2]
    base = me_ref[0] * block_count

    def one_block(block, carry):
        states = pl.ds(pl.multiple_of(block * tile_rows, tile_rows), tile_rows)
        for action in range(action_count):
            left, right = [], []
            for n in range(entry_count):
                rel = dest_ref[n, action, block] - base
                here = (n < counts_ref[action, block]) & (rel >= 0) & (rel < block_count)
                tile = tiles_ref[block, action, n]
                left.append(jnp.where(here, tile, jnp.zeros_like(tile)))
                right.append(value_ref[jnp.where(here, rel, 0)])
            cont = jnp.dot(
                jnp.concatenate(left, axis=1), jnp.concatenate(right, axis=0), preferred_element_type=jnp.float32
            )
            util = jnp.broadcast_to(util_ref[action : action + 1, states], (tile_rows, tile_rows)).T
            taste = taste_ref[action : action + 1, :]
            for c in range(0, width, tile_rows):
                cols = slice(c, c + tile_rows)
                out_ref[block, action, :, cols] = (util + taste[:, cols]) + DISCOUNT * cont[:, cols]
        return carry

    lax.fori_loop(0, block_count, one_block, 0)


def local_forward(me, dest, counts, value_blocks, tiles, state_util, taste, sent):
    block_count, action_count, _, tile_rows, _ = tiles.shape
    return pl.pallas_call(
        local_forward_kernel,
        out_shape=jax.ShapeDtypeStruct((block_count, action_count, tile_rows, value_blocks.shape[2]), jnp.float32),
        in_specs=[SMEM_SPEC] * 3 + [VMEM_SPEC] * 4 + [ANY_SPEC],
        out_specs=VMEM_SPEC,
        compiler_params=PARAMS,
        cost_estimate=SMALL_COST,
        name="local_forward",
    )(me, dest, counts, value_blocks, tiles, state_util, taste, sent)


def unpack(code):
    return code >> 8, (code >> 4) & 15, code & 15


def add_rows(source_ref, incoming_ref, tiles_ref, scores_ref):
    for k in range(incoming_ref.shape[0]):
        code = source_ref[0, k]
        block, action, n = unpack(jnp.maximum(code, 0))
        tile = tiles_ref[block, action, n]
        tile = jnp.where(code >= 0, tile, jnp.zeros_like(tile))
        scores_ref[block, action] += DISCOUNT * jnp.dot(tile, incoming_ref[k], preferred_element_type=jnp.float32)


def add_incoming_kernel(source_ref, incoming_ref, tiles_ref, scores_in_ref, scores_ref):
    del scores_in_ref
    add_rows(source_ref, incoming_ref, tiles_ref, scores_ref)


def add_incoming(source, incoming, tiles, scores):
    return pl.pallas_call(
        add_incoming_kernel,
        out_shape=jax.ShapeDtypeStruct(scores.shape, scores.dtype),
        in_specs=[SMEM_SPEC] + [VMEM_SPEC] * 3,
        out_specs=VMEM_SPEC,
        input_output_aliases={3: 0},
        compiler_params=PARAMS,
        cost_estimate=SMALL_COST,
        name="add_incoming",
    )(source, incoming, tiles, scores)


def soft_max(scores):
    largest = functools.reduce(jnp.maximum, scores)
    if len(scores) == 2:
        ahead = scores[0] >= scores[1]
        power = jnp.exp(-jnp.abs(scores[0] - scores[1]))
        return largest, [jnp.where(ahead, 1.0, power), jnp.where(ahead, power, 1.0)], 1.0 + power
    powers = [jnp.exp(x - largest) for x in scores]
    return largest, powers, functools.reduce(jnp.add, powers)


def transposed_dot(tile, rows):
    return lax.dot_general(tile, rows, (((0,), (0,)), ((), ())), preferred_element_type=jnp.float32)


def lead_terms_kernel(row_count, *refs):
    last_refs, incoming_refs = refs[:row_count], refs[row_count : 2 * row_count]
    source_ref, tiles_ref, cot_ref, _, scores_ref, out_ref, scaled_ref = refs[2 * row_count :]
    for last_ref, incoming_ref in zip(last_refs, incoming_refs):
        add_rows(last_ref, incoming_ref, tiles_ref, scores_ref)
    _, action_count, _, tile_rows, _ = tiles_ref.shape
    capacity = source_ref.shape[1]
    width = cot_ref.shape[2]

    def one_term(k, carry):
        code = source_ref[0, k]

        @pl.when(code >= 0)
        def _():
            block, action, n = unpack(code)
            for c in range(0, width, tile_rows):
                cols = slice(c, c + tile_rows)
                _, powers, total = soft_max([scores_ref[block, other, :, cols] for other in range(action_count)])
                power = powers[0]
                for other in range(1, action_count):
                    power = jnp.where(action == other, powers[other], power)
                grad = cot_ref[block, :, cols].astype(jnp.float32) / total * power
                scaled_ref[:, cols] = (DISCOUNT * grad).astype(jnp.bfloat16)
            rows = pl.ds(pl.multiple_of(k * tile_rows, tile_rows), tile_rows)
            out_ref[rows, :] = transposed_dot(tiles_ref[block, action, n], scaled_ref[...]).astype(jnp.bfloat16)

        return carry

    lax.fori_loop(0, capacity, one_term, 0)


def lead_terms(last, incoming, source, scores, tiles, cot_blocks, rows):
    tile_rows, width = tiles.shape[3], cot_blocks.shape[2]
    count = len(last)
    return pl.pallas_call(
        functools.partial(lead_terms_kernel, count),
        out_shape=(
            jax.ShapeDtypeStruct(scores.shape, scores.dtype),
            jax.ShapeDtypeStruct((rows, width), jnp.bfloat16),
        ),
        in_specs=[SMEM_SPEC] * count + [VMEM_SPEC] * count + [SMEM_SPEC] + [VMEM_SPEC] * 3,
        out_specs=(VMEM_SPEC, VMEM_SPEC),
        scratch_shapes=[pltpu.VMEM((tile_rows, width), jnp.bfloat16)],
        input_output_aliases={2 * count + 3: 0},
        compiler_params=PARAMS,
        cost_estimate=SMALL_COST,
        name="lead_terms",
    )(*last, *incoming, source, tiles, cot_blocks, scores)


def split_rows(x):
    high = x.astype(jnp.bfloat16)
    rest = x - high.astype(jnp.float32)
    middle = rest.astype(jnp.bfloat16)
    return high, middle, (rest - middle.astype(jnp.float32)).astype(jnp.bfloat16)


def join_rows(parts):
    high, middle, low = (x.astype(jnp.float32) for x in parts)
    return (high + middle) + low


def score_kernel(row_count, scales, *refs):
    source_refs = refs[:row_count]
    scores_ref, tiles_ref, cot_ref, _, value_ref, scaled_ref, util_ref, taste_ref = refs[row_count : row_count + 8]
    out_refs = refs[row_count + 8 :]
    util_scale, taste_scale = scales
    block = pl.program_id(0)
    _, action_count, tile_rows, width = scores_ref.shape
    states = pl.ds(pl.multiple_of(block * tile_rows, tile_rows), tile_rows)

    @pl.when(block == 0)
    def _():
        taste_ref[...] = jnp.zeros_like(taste_ref)

    sums = [jnp.zeros((tile_rows, tile_rows), jnp.float32) for _ in range(action_count)]
    for c in range(0, width, tile_rows):
        cols = slice(c, c + tile_rows)
        largest, powers, total = soft_max([scores_ref[block, action, :, cols] for action in range(action_count)])
        value_ref[:, cols] = largest + jnp.log(total)
        ratio = cot_ref[block, :, cols].astype(jnp.float32) / total
        for action in range(action_count):
            grad = ratio * powers[action]
            scaled_ref[block, action, :, cols] = (DISCOUNT * grad).astype(jnp.bfloat16)
            sums[action] = sums[action] + grad
            taste_ref[action : action + 1, cols] += taste_scale * jnp.sum(grad, axis=0, keepdims=True)
    for action in range(action_count):
        util_ref[action : action + 1, states] = util_scale * jnp.sum(sums[action].T, axis=0, keepdims=True)

    @pl.when(block == pl.num_programs(0) - 1)
    def _():
        for source_ref, out_ref in zip(source_refs, out_refs):
            capacity = source_ref.shape[1]

            def one_term(k, carry):
                code = source_ref[0, k]

                @pl.when(code >= 0)
                def _():
                    block, action, n = unpack(code)
                    rows = pl.ds(pl.multiple_of(k * tile_rows, tile_rows), tile_rows)
                    out_ref[rows, :] = transposed_dot(tiles_ref[block, action, n], scaled_ref[block, action]).astype(
                        jnp.bfloat16
                    )

                return carry

            lax.fori_loop(0, capacity, one_term, 0)
            rows = list(split_rows(taste_ref[...]))
            spare = out_ref.shape[0] - capacity * tile_rows - sum(x.shape[0] for x in rows)
            rows.append(jnp.zeros((spare, width), jnp.bfloat16))
            out_ref[capacity * tile_rows :, :] = jnp.concatenate(rows, axis=0)


def score(sources, scores, tiles, cot_blocks, sent, scales, rows):
    block_count, action_count, tile_rows, width = scores.shape
    states = block_count * tile_rows
    return pl.pallas_call(
        functools.partial(score_kernel, len(sources), scales),
        out_shape=[
            jax.ShapeDtypeStruct((states, width), jnp.float32),
            jax.ShapeDtypeStruct(scores.shape, jnp.bfloat16),
            jax.ShapeDtypeStruct((action_count, states), jnp.float32),
            jax.ShapeDtypeStruct((action_count, width), jnp.float32),
        ]
        + [jax.ShapeDtypeStruct((rows, width), jnp.bfloat16)] * len(sources),
        grid=(block_count,),
        in_specs=[SMEM_SPEC] * len(sources) + [VMEM_SPEC] * 3 + [ANY_SPEC],
        out_specs=[pl.BlockSpec((tile_rows, width), lambda i: (i, 0))] + [VMEM_SPEC] * (3 + len(sources)),
        compiler_params=PARAMS,
        cost_estimate=SMALL_COST,
        name="score",
    )(*sources, scores, tiles, cot_blocks, sent)


def local_adjoint_kernel(me_ref, dest_ref, counts_ref, tiles_ref, scaled_ref, sent_ref, held_ref, written_ref, sem):
    del sent_ref
    block_count, action_count, entry_count, _, _ = tiles_ref.shape
    base = me_ref[0] * block_count

    def clear(block, carry):
        held_ref[block] = jnp.zeros_like(held_ref[block])
        return carry

    lax.fori_loop(0, block_count, clear, 0)

    def one_block(block, carry):
        for action in range(action_count):
            for n in range(entry_count):
                rel = dest_ref[n, action, block] - base
                here = (n < counts_ref[action, block]) & (rel >= 0) & (rel < block_count)
                tile = tiles_ref[block, action, n]
                tile = jnp.where(here, tile, jnp.zeros_like(tile))
                held_ref[jnp.where(here, rel, 0)] += transposed_dot(tile, scaled_ref[block, action])
        return carry

    lax.fori_loop(0, block_count, one_block, 0)
    copy = pltpu.make_async_copy(held_ref, written_ref, sem)
    copy.start()
    copy.wait()


def local_adjoint(me, dest, counts, tiles, scaled, sent):
    block_count, _, _, tile_rows, _ = tiles.shape
    shape = jax.ShapeDtypeStruct((block_count, tile_rows, scaled.shape[3]), jnp.float32)
    return pl.pallas_call(
        local_adjoint_kernel,
        out_shape=(shape, shape),
        in_specs=[SMEM_SPEC] * 3 + [VMEM_SPEC] * 2 + [ANY_SPEC],
        out_specs=(VMEM_SPEC, HBM_SPEC),
        scratch_shapes=[pltpu.SemaphoreType.DMA],
        compiler_params=PARAMS,
        cost_estimate=SMALL_COST,
        name="local_adjoint",
    )(me, dest, counts, tiles, scaled, sent)


def add_arrivals_kernel(count, taste_offsets, *refs):
    wanted_refs, arrived_refs = refs[:count], refs[count : 2 * count]
    rest = refs[2 * count + 2 :]
    if taste_offsets:
        me_ref, lead_ref, own_ref, held_ref, written_ref, taste_ref, sems, part_ref = rest
    else:
        held_ref, written_ref, sems = rest
    slots = wanted_refs[0].shape[1]
    tile_rows = held_ref.shape[1]
    target = [ref[0, k] for ref in wanted_refs for k in range(slots)]
    total = len(target)
    place = [jnp.maximum(t, 0) for t in target]
    store = [pltpu.make_async_copy(held_ref.at[place[k]], written_ref.at[place[k]], sems.at[k]) for k in range(total)]
    last = []
    for k in range(total):
        final = target[k] >= 0
        for other in range(k + 1, total):
            final = final & (target[other] != target[k])
        last.append(final)
    for k in range(total):

        @pl.when(target[k] >= 0)
        def _():
            first = k % slots * tile_rows
            held_ref[place[k]] += arrived_refs[k // slots][first : first + tile_rows, :].astype(jnp.float32)

        @pl.when(last[k])
        def _():
            store[k].start()

    if taste_offsets:
        devices, action_count = part_ref.shape[:2]
        me = me_ref[0]

        def sender(offset):
            return lax.rem(me - offset + devices, devices)

        part_ref[me] = own_ref[...]
        part_ref[sender(taste_offsets[0])] = lead_ref[...]
        for offset, arrived_ref in zip(taste_offsets[1:], arrived_refs):
            first = [slots * tile_rows + p * action_count for p in range(3)]
            part_ref[sender(offset)] = join_rows([arrived_ref[f : f + action_count, :] for f in first])
        taste = part_ref[0]
        for device in range(1, devices):
            taste = taste + part_ref[device]
        taste_ref[...] = taste

    for k in range(total):

        @pl.when(last[k])
        def _():
            store[k].wait()


def add_arrivals(wanted, arrived, held, written, taste=()):
    count = len(wanted)
    shape = jax.ShapeDtypeStruct(held.shape, held.dtype)
    out_shape, out_specs = [shape, shape], [VMEM_SPEC, HBM_SPEC]
    in_specs = [SMEM_SPEC] * count + [VMEM_SPEC] * (count + 1) + [HBM_SPEC]
    scratch = [pltpu.SemaphoreType.DMA((count * wanted[0].shape[1],))]
    offsets, extra = (), ()
    if taste:
        offsets, extra = tuple(taste[0]), taste[1:]
        own = extra[-1]
        out_shape.append(jax.ShapeDtypeStruct(own.shape, own.dtype))
        out_specs.append(VMEM_SPEC)
        in_specs += [SMEM_SPEC] + [VMEM_SPEC] * 2
        scratch.append(pltpu.VMEM((len(offsets) + 1,) + own.shape, own.dtype))
    return pl.pallas_call(
        functools.partial(add_arrivals_kernel, count, offsets),
        out_shape=out_shape,
        in_specs=in_specs,
        out_specs=out_specs,
        scratch_shapes=scratch,
        input_output_aliases={2 * count: 0, 2 * count + 1: 1},
        compiler_params=PARAMS,
        cost_estimate=SMALL_COST,
        name="add_arrivals",
    )(*wanted, *arrived, held, written, *extra)


def local(value_in, cotangent, state_util, taste, tiles, dest_block, counts):
    block_count, action_count, _, tile_rows, _ = tiles.shape
    states, width = value_in.shape
    device_count = lax.axis_size("state")
    me = lax.axis_index("state").astype(jnp.int32).reshape(1)
    capacity = max(2, (block_count + device_count - 2) // (device_count - 1))
    value_blocks = value_in.reshape(block_count, tile_rows, width)
    cot_blocks = cotangent.reshape(block_count, tile_rows, width)
    offsets = range(1, device_count)
    order = sorted(offsets, key=lambda d: -min(d, device_count - d))

    def shift(x, offset):
        return lax.ppermute(x, "state", [(s, (s + offset) % device_count) for s in range(device_count)])

    def add_over(x, axis):
        size = lax.axis_size(axis)
        if size & (size - 1):
            return lax.psum(x, axis)
        step = 1
        while step < size:
            x = x + lax.ppermute(x, axis, [(s, s ^ step) for s in range(size)])
            step *= 2
        return x

    dest, counts = dest_block.transpose(2, 1, 0), counts.T
    request, source = make_plan(me, dest, counts, device_count, capacity)
    wanted = {d: shift(request[d - 1], d) for d in order}
    staged = stage(value_blocks, request[0])
    outgoing = {d: gather_blocks(wanted[d], staged) for d in order}
    incoming = {d: shift(outgoing[d], -d) for d in order}
    scores = local_forward(me, dest, counts, staged, tiles, state_util, taste, outgoing[order[-1]])
    early, late = order[:1], order[1:]
    for d in early:
        scores = add_incoming(source[d - 1], incoming[d], tiles, scores)

    rows = capacity * tile_rows + 16 * pl.cdiv(3 * action_count, 16)
    scores, lead = lead_terms(
        [source[d - 1] for d in late], [incoming[d] for d in late], source[order[0] - 1], scores, tiles, cot_blocks, rows
    )
    scales = (1.0 / (width * lax.axis_size("type")), 1.0 / (states * device_count))
    value_out, scaled, util_part, taste_part, *rest = score(
        [source[d - 1] for d in late], scores, tiles, cot_blocks, lead, scales, rows
    )
    terms = [lead, *rest]
    returned = [shift(x, d) for d, x in zip(order, terms)]
    lead_taste = shift(taste_part, order[0])
    held, written = local_adjoint(me, dest, counts, tiles, scaled, terms[-1])
    util_total = add_over(util_part, "type")
    held, written = add_arrivals([wanted[order[0]]], returned[:1], held, written)
    held, written, taste_total = add_arrivals(
        [wanted[d] for d in late], returned[1:], held, written, (order, me, lead_taste, taste_part)
    )
    return value_out, written.reshape(states, width), util_total, taste_total


def solution(mesh):
    return jax.shard_map(
        local,
        mesh=mesh,
        in_specs=(
            P(("groups", "state"), "type"),
            P(("groups", "state"), "type"),
            P(None, ("groups", "state")),
            P(None, ("groups", "type")),
            P(("groups", "state"), None, None, None, None),
            P(("groups", "state"), None, None),
            P(("groups", "state"), None),
        ),
        out_specs=(
            P(("groups", "state"), "type"),
            P(("groups", "state"), "type"),
            P(None, ("groups", "state")),
            P(None, ("groups", "type")),
        ),
        check_vma=False,
    )
```

```python
import functools

import jax
import jax.numpy as jnp
from jax import lax
from jax.experimental import pallas as pl
from jax.experimental.pallas import tpu as pltpu
from jax.sharding import PartitionSpec as P

DISCOUNT = 0.95
VMEM_LIMIT = 12 * 1024 * 1024

SMEM_SPEC = pl.BlockSpec(memory_space=pltpu.SMEM)
ANY_SPEC = pl.BlockSpec(memory_space=pl.ANY)
HBM_SPEC = pl.BlockSpec(memory_space=pltpu.HBM)
VMEM_SPEC = pl.BlockSpec(memory_space=pltpu.VMEM)
PARAMS = pltpu.CompilerParams(vmem_limit_bytes=VMEM_LIMIT)
PLAN_COST = pl.CostEstimate(flops=2 * 10**10, bytes_accessed=1000, transcendentals=0)
SMALL_COST = pl.CostEstimate(flops=1000, bytes_accessed=1000, transcendentals=0)


def dot_counts(x, y, contract=(1, 0)):
    return lax.dot_general(
        x.astype(jnp.float32).astype(jnp.bfloat16), y.astype(jnp.float32).astype(jnp.bfloat16),
        (((contract[0],), (contract[1],)), ((), ())), preferred_element_type=jnp.float32,
    )


def iota(shape, dim):
    return lax.broadcasted_iota(jnp.int32, shape, dim)


def plan_kernel(device_count, me_ref, dest_ref, *refs):
    request_refs = refs[: device_count - 1]
    source_refs = refs[device_count - 1 : 2 * (device_count - 1)]
    mark_ref, local_ref = refs[2 * (device_count - 1) :]
    entry_count, action_count, block_count = dest_ref.shape
    capacity = request_refs[0].shape[1]
    places = 8 * pl.cdiv(capacity, 8)
    me = me_ref[0]
    mark_ref[...] = jnp.zeros_like(mark_ref)
    local_ref[...] = jnp.zeros_like(local_ref)
    for n in range(entry_count):
        dest = dest_ref[n]
        owner = jnp.zeros_like(dest)
        for other in range(1, device_count):
            owner += (dest >= other * block_count).astype(jnp.int32)
        offset = owner - me
        offset = jnp.where(offset < 0, offset + device_count, offset)
        mark_ref[n * action_count : (n + 1) * action_count, :] = offset
        local_ref[n * action_count : (n + 1) * action_count, :] = dest - owner * block_count
    mark, local = mark_ref[...], local_ref[...]
    row, lane = iota(mark.shape, 0), iota(mark.shape, 1)
    square = (block_count, block_count)
    before = iota(square, 0) < iota(square, 1)
    whole = jnp.ones(square, jnp.int32)
    tall = (mark.shape[0],) * 2
    above = iota(tall, 1) < iota(tall, 0)
    ones = jnp.ones((8, block_count), jnp.int32)
    place_iota = iota((places, block_count), 0)
    for offset in range(1, device_count):
        hit = mark == offset
        place = (dot_counts(hit, before) + dot_counts(above, dot_counts(hit, whole))).astype(jnp.int32)
        place = jnp.where(hit, place, -1)
        wants = jnp.zeros((places, block_count), jnp.int32)
        blocks = jnp.zeros((places, block_count), jnp.int32)
        lists = jnp.zeros((places, block_count), jnp.int32)
        for r in range(entry_count * action_count):
            here = place[r : r + 1, :] == place_iota
            wants = jnp.where(here, local[r : r + 1, :] + 1, wants)
            blocks = jnp.where(here, lane[r : r + 1, :], blocks)
            lists = jnp.where(here, row[r : r + 1, :], lists)
        wants, blocks, lists = (dot_counts(ones, x, (1, 1)).astype(jnp.int32) for x in (wants, blocks, lists))
        entry = lists // action_count
        codes = jnp.where(wants > 0, blocks * 256 + (lists - entry * action_count) * 16 + entry, -1)
        request_refs[offset - 1][...] = (wants - 1)[:1, :capacity]
        source_refs[offset - 1][...] = codes[:1, :capacity]


def make_plan(me, dest, device_count, capacity):
    entry_count, action_count, block_count = dest.shape
    padded = 8 * pl.cdiv(entry_count * action_count, 8)
    outs = pl.pallas_call(
        functools.partial(plan_kernel, device_count),
        out_shape=[jax.ShapeDtypeStruct((1, capacity), jnp.int32)] * (2 * (device_count - 1)),
        in_specs=[SMEM_SPEC, VMEM_SPEC],
        out_specs=[VMEM_SPEC] * (2 * (device_count - 1)),
        scratch_shapes=[pltpu.VMEM((padded, block_count), jnp.int32)] * 2,
        compiler_params=PARAMS,
        cost_estimate=PLAN_COST,
        name="plan",
    )(me, dest)
    return outs[: device_count - 1], outs[device_count - 1 :]


def stage_kernel(value_ref, plan_ref, out_ref):
    del plan_ref
    for block in range(out_ref.shape[0]):
        out_ref[block] = value_ref[block]


def stage(value_blocks, plan):
    return pl.pallas_call(
        stage_kernel,
        out_shape=jax.ShapeDtypeStruct(value_blocks.shape, value_blocks.dtype),
        in_specs=[VMEM_SPEC, ANY_SPEC],
        out_specs=VMEM_SPEC,
        compiler_params=PARAMS,
        cost_estimate=SMALL_COST,
        name="stage",
    )(value_blocks, plan)


def gather_kernel(wanted_ref, value_ref, out_ref):
    for k in range(out_ref.shape[0]):
        out_ref[k] = value_ref[jnp.maximum(wanted_ref[0, k], 0)]


def gather_blocks(wanted, value_blocks):
    return pl.pallas_call(
        gather_kernel,
        out_shape=jax.ShapeDtypeStruct(wanted.shape[1:] + value_blocks.shape[1:], value_blocks.dtype),
        in_specs=[SMEM_SPEC, VMEM_SPEC],
        out_specs=VMEM_SPEC,
        compiler_params=PARAMS,
        cost_estimate=SMALL_COST,
        name="gather",
    )(wanted, value_blocks)


def local_forward_kernel(me_ref, dest_ref, counts_ref, value_ref, tiles_ref, util_ref, taste_ref, sent_ref, out_ref):
    del sent_ref
    block_count, action_count, entry_count, tile_rows, _ = tiles_ref.shape
    width = value_ref.shape[2]
    base = me_ref[0] * block_count

    def one_block(block, carry):
        states = pl.ds(pl.multiple_of(block * tile_rows, tile_rows), tile_rows)
        for action in range(action_count):
            left, right = [], []
            for n in range(entry_count):
                rel = dest_ref[n, action, block] - base
                here = (n < counts_ref[action, block]) & (rel >= 0) & (rel < block_count)
                tile = tiles_ref[block, action, n]
                left.append(jnp.where(here, tile, jnp.zeros_like(tile)))
                right.append(value_ref[jnp.where(here, rel, 0)])
            cont = jnp.dot(
                jnp.concatenate(left, axis=1), jnp.concatenate(right, axis=0), preferred_element_type=jnp.float32
            )
            util = jnp.broadcast_to(util_ref[action : action + 1, states], (tile_rows, tile_rows)).T
            taste = taste_ref[action : action + 1, :]
            for c in range(0, width, tile_rows):
                cols = slice(c, c + tile_rows)
                out_ref[block, action, :, cols] = (util + taste[:, cols]) + DISCOUNT * cont[:, cols]
        return carry

    lax.fori_loop(0, block_count, one_block, 0)


def local_forward(me, dest, counts, value_blocks, tiles, state_util, taste, sent):
    block_count, action_count, _, tile_rows, _ = tiles.shape
    return pl.pallas_call(
        local_forward_kernel,
        out_shape=jax.ShapeDtypeStruct((block_count, action_count, tile_rows, value_blocks.shape[2]), jnp.float32),
        in_specs=[SMEM_SPEC] * 3 + [VMEM_SPEC] * 4 + [ANY_SPEC],
        out_specs=VMEM_SPEC,
        compiler_params=PARAMS,
        cost_estimate=SMALL_COST,
        name="local_forward",
    )(me, dest, counts, value_blocks, tiles, state_util, taste, sent)


def unpack(code):
    return code >> 8, (code >> 4) & 15, code & 15


def add_rows(source_ref, incoming_ref, tiles_ref, scores_ref):
    for k in range(incoming_ref.shape[0]):
        code = source_ref[0, k]
        block, action, n = unpack(jnp.maximum(code, 0))
        tile = tiles_ref[block, action, n]
        tile = jnp.where(code >= 0, tile, jnp.zeros_like(tile))
        scores_ref[block, action] += DISCOUNT * jnp.dot(tile, incoming_ref[k], preferred_element_type=jnp.float32)


def add_incoming_kernel(source_ref, incoming_ref, tiles_ref, scores_in_ref, scores_ref):
    del scores_in_ref
    add_rows(source_ref, incoming_ref, tiles_ref, scores_ref)


def add_incoming(source, incoming, tiles, scores):
    return pl.pallas_call(
        add_incoming_kernel,
        out_shape=jax.ShapeDtypeStruct(scores.shape, scores.dtype),
        in_specs=[SMEM_SPEC] + [VMEM_SPEC] * 3,
        out_specs=VMEM_SPEC,
        input_output_aliases={3: 0},
        compiler_params=PARAMS,
        cost_estimate=SMALL_COST,
        name="add_incoming",
    )(source, incoming, tiles, scores)


def reciprocal(x):
    guess = pl.reciprocal(x, approx=True)
    return guess * (2.0 - x * guess)


def soft_max(scores):
    largest = functools.reduce(jnp.maximum, scores)
    if len(scores) == 2:
        ahead = scores[0] >= scores[1]
        power = jnp.exp(-jnp.abs(scores[0] - scores[1]))
        return largest, [jnp.where(ahead, 1.0, power), jnp.where(ahead, power, 1.0)], 1.0 + power
    powers = [jnp.exp(x - largest) for x in scores]
    return largest, powers, functools.reduce(jnp.add, powers)


def transposed_dot(tile, rows):
    return lax.dot_general(tile, rows, (((0,), (0,)), ((), ())), preferred_element_type=jnp.float32)


def lead_terms_kernel(row_count, *refs):
    last_refs, incoming_refs = refs[:row_count], refs[row_count : 2 * row_count]
    source_ref, tiles_ref, cot_ref, _, scores_ref, out_ref, scaled_ref = refs[2 * row_count :]
    for last_ref, incoming_ref in zip(last_refs, incoming_refs):
        add_rows(last_ref, incoming_ref, tiles_ref, scores_ref)
    _, action_count, _, tile_rows, _ = tiles_ref.shape
    capacity = source_ref.shape[1]
    width = cot_ref.shape[2]

    def one_term(k, carry):
        block, action, n = unpack(jnp.maximum(source_ref[0, k], 0))
        for c in range(0, width, tile_rows):
            cols = slice(c, c + tile_rows)
            if action_count == 2:
                behind = scores_ref[block, 1 - action, :, cols] - scores_ref[block, action, :, cols]
                power = jnp.exp(-jnp.abs(behind))
                total, power = 1.0 + power, jnp.where(behind > 0, power, 1.0)
            else:
                _, powers, total = soft_max([scores_ref[block, other, :, cols] for other in range(action_count)])
                power = powers[0]
                for other in range(1, action_count):
                    power = jnp.where(action == other, powers[other], power)
            grad = cot_ref[block, :, cols].astype(jnp.float32) * reciprocal(total) * power
            scaled_ref[:, cols] = (DISCOUNT * grad).astype(jnp.bfloat16)
        rows = pl.ds(pl.multiple_of(k * tile_rows, tile_rows), tile_rows)
        out_ref[rows, :] = transposed_dot(tiles_ref[block, action, n], scaled_ref[...]).astype(jnp.bfloat16)
        return carry

    lax.fori_loop(0, capacity, one_term, 0)


def lead_terms(last, incoming, source, scores, tiles, cot_blocks, rows):
    tile_rows, width = tiles.shape[3], cot_blocks.shape[2]
    count = len(last)
    return pl.pallas_call(
        functools.partial(lead_terms_kernel, count),
        out_shape=(
            jax.ShapeDtypeStruct(scores.shape, scores.dtype),
            jax.ShapeDtypeStruct((rows, width), jnp.bfloat16),
        ),
        in_specs=[SMEM_SPEC] * count + [VMEM_SPEC] * count + [SMEM_SPEC] + [VMEM_SPEC] * 3,
        out_specs=(VMEM_SPEC, VMEM_SPEC),
        scratch_shapes=[pltpu.VMEM((tile_rows, width), jnp.bfloat16)],
        input_output_aliases={2 * count + 3: 0},
        compiler_params=PARAMS,
        cost_estimate=SMALL_COST,
        name="lead_terms",
    )(*last, *incoming, source, tiles, cot_blocks, scores)


def split_rows(x):
    high = x.astype(jnp.bfloat16)
    rest = x - high.astype(jnp.float32)
    middle = rest.astype(jnp.bfloat16)
    return high, middle, (rest - middle.astype(jnp.float32)).astype(jnp.bfloat16)


def join_rows(parts):
    high, middle, low = (x.astype(jnp.float32) for x in parts)
    return (high + middle) + low


def score_kernel(row_count, scales, *refs):
    source_refs = refs[:row_count]
    scores_ref, tiles_ref, cot_ref, _, value_ref, scaled_ref, util_ref, taste_ref = refs[row_count : row_count + 8]
    out_refs, (held_ref, sems) = refs[row_count + 8 : -2], refs[-2:]
    util_scale, taste_scale = scales
    block_count, action_count, tile_rows, width = scores_ref.shape
    taste_ref[...] = jnp.zeros_like(taste_ref)

    def states(block):
        return pl.ds(pl.multiple_of(block * tile_rows, tile_rows), tile_rows)

    def store(block):
        return pltpu.make_async_copy(held_ref.at[block], value_ref.at[states(block), :], sems.at[block])

    def one_block(block, carry):
        sums = [jnp.zeros((tile_rows, tile_rows), jnp.float32) for _ in range(action_count)]
        for c in range(0, width, tile_rows):
            cols = slice(c, c + tile_rows)
            largest, powers, total = soft_max([scores_ref[block, action, :, cols] for action in range(action_count)])
            held_ref[block, :, cols] = largest + jnp.log(total)
            ratio = cot_ref[block, :, cols].astype(jnp.float32) * reciprocal(total)
            for action in range(action_count):
                grad = ratio * powers[action]
                scaled_ref[block, action, :, cols] = (DISCOUNT * grad).astype(jnp.bfloat16)
                sums[action] = sums[action] + grad
                taste_ref[action : action + 1, cols] += taste_scale * jnp.sum(grad, axis=0, keepdims=True)
        store(block).start()
        for action in range(action_count):
            util_ref[action : action + 1, states(block)] = util_scale * jnp.sum(sums[action].T, axis=0, keepdims=True)
        return carry

    lax.fori_loop(0, block_count, one_block, 0)
    for source_ref, out_ref in zip(source_refs, out_refs):
        capacity = source_ref.shape[1]
        for k in range(capacity):
            block, action, n = unpack(jnp.maximum(source_ref[0, k], 0))
            out_ref[k * tile_rows : (k + 1) * tile_rows, :] = transposed_dot(
                tiles_ref[block, action, n], scaled_ref[block, action]
            ).astype(jnp.bfloat16)
        rows = list(split_rows(taste_ref[...]))
        spare = out_ref.shape[0] - capacity * tile_rows - sum(x.shape[0] for x in rows)
        rows.append(jnp.zeros((spare, width), jnp.bfloat16))
        out_ref[capacity * tile_rows :, :] = jnp.concatenate(rows, axis=0)
    for block in range(block_count):
        store(block).wait()


def score(sources, scores, tiles, cot_blocks, sent, scales, rows):
    block_count, action_count, tile_rows, width = scores.shape
    states = block_count * tile_rows
    return pl.pallas_call(
        functools.partial(score_kernel, len(sources), scales),
        out_shape=[
            jax.ShapeDtypeStruct((states, width), jnp.float32),
            jax.ShapeDtypeStruct(scores.shape, jnp.bfloat16),
            jax.ShapeDtypeStruct((action_count, states), jnp.float32),
            jax.ShapeDtypeStruct((action_count, width), jnp.float32),
        ]
        + [jax.ShapeDtypeStruct((rows, width), jnp.bfloat16)] * len(sources),
        in_specs=[SMEM_SPEC] * len(sources) + [VMEM_SPEC] * 3 + [ANY_SPEC],
        out_specs=[HBM_SPEC] + [VMEM_SPEC] * (3 + len(sources)),
        scratch_shapes=[
            pltpu.VMEM((block_count, tile_rows, width), jnp.float32),
            pltpu.SemaphoreType.DMA((block_count,)),
        ],
        compiler_params=PARAMS,
        cost_estimate=SMALL_COST,
        name="score",
    )(*sources, scores, tiles, cot_blocks, sent)


def local_adjoint_kernel(me_ref, dest_ref, counts_ref, tiles_ref, scaled_ref, sent_ref, held_ref, written_ref, sem):
    del sent_ref
    block_count, action_count, entry_count, _, _ = tiles_ref.shape
    base = me_ref[0] * block_count

    def clear(block, carry):
        held_ref[block] = jnp.zeros_like(held_ref[block])
        return carry

    lax.fori_loop(0, block_count, clear, 0)

    def one_block(block, carry):
        for action in range(action_count):
            for n in range(entry_count):
                rel = dest_ref[n, action, block] - base
                here = (n < counts_ref[action, block]) & (rel >= 0) & (rel < block_count)
                tile = tiles_ref[block, action, n]
                tile = jnp.where(here, tile, jnp.zeros_like(tile))
                held_ref[jnp.where(here, rel, 0)] += transposed_dot(tile, scaled_ref[block, action])
        return carry

    lax.fori_loop(0, block_count, one_block, 0)
    copy = pltpu.make_async_copy(held_ref, written_ref, sem)
    copy.start()
    copy.wait()


def local_adjoint(me, dest, counts, tiles, scaled, sent):
    block_count, _, _, tile_rows, _ = tiles.shape
    shape = jax.ShapeDtypeStruct((block_count, tile_rows, scaled.shape[3]), jnp.float32)
    return pl.pallas_call(
        local_adjoint_kernel,
        out_shape=(shape, shape),
        in_specs=[SMEM_SPEC] * 3 + [VMEM_SPEC] * 2 + [ANY_SPEC],
        out_specs=(VMEM_SPEC, HBM_SPEC),
        scratch_shapes=[pltpu.SemaphoreType.DMA],
        compiler_params=PARAMS,
        cost_estimate=SMALL_COST,
        name="local_adjoint",
    )(me, dest, counts, tiles, scaled, sent)


def add_arrivals_kernel(count, taste_offsets, *refs):
    wanted_refs, arrived_refs = refs[:count], refs[count : 2 * count]
    rest = refs[2 * count + 2 :]
    if taste_offsets:
        me_ref, lead_ref, own_ref, held_ref, written_ref, taste_ref, sems, part_ref = rest
    else:
        held_ref, written_ref, sems = rest
    slots = wanted_refs[0].shape[1]
    tile_rows = held_ref.shape[1]
    target = [ref[0, k] for ref in wanted_refs for k in range(slots)]
    total = len(target)
    place = [jnp.maximum(t, 0) for t in target]
    store = [pltpu.make_async_copy(held_ref.at[place[k]], written_ref.at[place[k]], sems.at[k]) for k in range(total)]
    last = []
    for k in range(total):
        final = target[k] >= 0
        for other in range(k + 1, total):
            final = final & (target[other] != target[k])
        last.append(final)
    for k in range(total):

        @pl.when(target[k] >= 0)
        def _():
            first = k % slots * tile_rows
            held_ref[place[k]] += arrived_refs[k // slots][first : first + tile_rows, :].astype(jnp.float32)

        @pl.when(last[k])
        def _():
            store[k].start()

    if taste_offsets:
        devices, action_count = part_ref.shape[:2]
        me = me_ref[0]

        def sender(offset):
            return lax.rem(me - offset + devices, devices)

        part_ref[me] = own_ref[...]
        part_ref[sender(taste_offsets[0])] = lead_ref[...]
        for offset, arrived_ref in zip(taste_offsets[1:], arrived_refs):
            first = [slots * tile_rows + p * action_count for p in range(3)]
            part_ref[sender(offset)] = join_rows([arrived_ref[f : f + action_count, :] for f in first])
        taste = part_ref[0]
        for device in range(1, devices):
            taste = taste + part_ref[device]
        taste_ref[...] = taste

    for k in range(total):

        @pl.when(last[k])
        def _():
            store[k].wait()


def add_arrivals(wanted, arrived, held, written, taste=()):
    count = len(wanted)
    shape = jax.ShapeDtypeStruct(held.shape, held.dtype)
    out_shape, out_specs = [shape, shape], [VMEM_SPEC, HBM_SPEC]
    in_specs = [SMEM_SPEC] * count + [VMEM_SPEC] * (count + 1) + [HBM_SPEC]
    scratch = [pltpu.SemaphoreType.DMA((count * wanted[0].shape[1],))]
    offsets, extra = (), ()
    if taste:
        offsets, extra = tuple(taste[0]), taste[1:]
        own = extra[-1]
        out_shape.append(jax.ShapeDtypeStruct(own.shape, own.dtype))
        out_specs.append(VMEM_SPEC)
        in_specs += [SMEM_SPEC] + [VMEM_SPEC] * 2
        scratch.append(pltpu.VMEM((len(offsets) + 1,) + own.shape, own.dtype))
    return pl.pallas_call(
        functools.partial(add_arrivals_kernel, count, offsets),
        out_shape=out_shape,
        in_specs=in_specs,
        out_specs=out_specs,
        scratch_shapes=scratch,
        input_output_aliases={2 * count: 0, 2 * count + 1: 1},
        compiler_params=PARAMS,
        cost_estimate=SMALL_COST,
        name="add_arrivals",
    )(*wanted, *arrived, held, written, *extra)


def local(value_in, cotangent, state_util, taste, tiles, dest_block, counts):
    block_count, action_count, _, tile_rows, _ = tiles.shape
    states, width = value_in.shape
    device_count = lax.axis_size("state")
    me = lax.axis_index("state").astype(jnp.int32).reshape(1)
    capacity = max(2, (block_count + device_count - 2) // (device_count - 1))
    value_blocks = value_in.reshape(block_count, tile_rows, width)
    cot_blocks = cotangent.reshape(block_count, tile_rows, width)
    offsets = range(1, device_count)
    order = sorted(offsets, key=lambda d: -min(d, device_count - d))

    def shift(x, offset):
        return lax.ppermute(x, "state", [(s, (s + offset) % device_count) for s in range(device_count)])

    def add_over(x, axis):
        size = lax.axis_size(axis)
        if size & (size - 1):
            return lax.psum(x, axis)
        step = 1
        while step < size:
            x = x + lax.ppermute(x, axis, [(s, s ^ step) for s in range(size)])
            step *= 2
        return x

    dest, counts = dest_block.transpose(2, 1, 0), counts.T
    request, source = make_plan(me, dest, device_count, capacity)
    wanted = {d: shift(request[d - 1], d) for d in order}
    staged = stage(value_blocks, request[0])
    outgoing = {d: gather_blocks(wanted[d], staged) for d in order}
    incoming = {d: shift(outgoing[d], -d) for d in order}
    scores = local_forward(me, dest, counts, staged, tiles, state_util, taste, outgoing[order[-1]])
    early, late = order[:1], order[1:]
    for d in early:
        scores = add_incoming(source[d - 1], incoming[d], tiles, scores)

    rows = capacity * tile_rows + 16 * pl.cdiv(3 * action_count, 16)
    scores, lead = lead_terms(
        [source[d - 1] for d in late], [incoming[d] for d in late], source[order[0] - 1], scores, tiles, cot_blocks, rows
    )
    scales = (1.0 / (width * lax.axis_size("type")), 1.0 / (states * device_count))
    value_out, scaled, util_part, taste_part, *rest = score(
        [source[d - 1] for d in late], scores, tiles, cot_blocks, lead, scales, rows
    )
    terms = [lead, *rest]
    returned = [shift(x, d) for d, x in zip(order, terms)]
    lead_taste = shift(taste_part, order[0])
    held, written = local_adjoint(me, dest, counts, tiles, scaled, terms[-1])
    util_total = add_over(util_part, "type")
    held, written = add_arrivals([wanted[order[0]]], returned[:1], held, written)
    held, written, taste_total = add_arrivals(
        [wanted[d] for d in late], returned[1:], held, written, (order, me, lead_taste, taste_part)
    )
    return value_out, written.reshape(states, width), util_total, taste_total


def solution(mesh):
    return jax.shard_map(
        local,
        mesh=mesh,
        in_specs=(
            P(("groups", "state"), "type"),
            P(("groups", "state"), "type"),
            P(None, ("groups", "state")),
            P(None, ("groups", "type")),
            P(("groups", "state"), None, None, None, None),
            P(("groups", "state"), None, None),
            P(("groups", "state"), None),
        ),
        out_specs=(
            P(("groups", "state"), "type"),
            P(("groups", "state"), "type"),
            P(None, ("groups", "state")),
            P(None, ("groups", "type")),
        ),
        check_vma=False,
    )
```
